256 devices in a mesh: pipe: 8 (over z), dp: 32 (over y, x, core).
Axes of the slice: x: 4, y: 4, z: 8, core: 2. Of those that a mesh axis runs over, the one named last changes fastest.
Arguments:
- acts: bfloat16 [32768, 6144], P(('pipe', 'dp'))
- grads_out: bfloat16 [32768, 24576], P(('pipe', 'dp')), may hold values from -6 to 6
- weight_grad: bfloat16 [6144, 24576], P('pipe', 'dp'), may hold values from -6 to 6
- slot_table: int32 [256], replicated, may hold values from -1 to 239, as said below
- row_counts: int32 [256], P(('pipe', 'dp')), may hold values from 32 to 128
- old_cov: float32 [32, 8, 128, 128], P('dp', 'pipe'), as said below
Outputs:
- precond_grad: bfloat16 [6144, 24576], P('pipe', 'dp')
- new_cov: float32 [32, 8, 128, 128], P('dp', 'pipe')
The draws below stay inside these ranges and needn't reach their ends.
Inputs may be any that keep to these rules, and one draw needn't show every extreme that they name: `slot_table`: every block 0 to 239 stands in exactly one slot; the other slots hold -1. `old_cov`: each block is symmetric and its diagonal dominates its row.
All inputs are finite; a program needn't handle non-finite values.
Results may differ from the reference program's by a relative error of at most 0.0045.
The reference program's roundings to bfloat16 on the way (of `inverse` and `left`) count: a program that leaves them out, or rounds other values in their place, can miss the bound.
Values may be sent and summed in bfloat16 or wider, within the bound.
No kernel may reach another device: no remote copies, remote signals or barrier semaphores. Data moves between devices by JAX's collectives and lax.ppermute only.
A program may use at most 128 MiB of HBM per device.

```python
import math
import jax
import jax.numpy as jnp
from jax import lax

D = 6144
FF = 24576
B = 128
TOK_DEV = 128
TOKENS = 32768
NA = 48
NG = 192
NBLK = 240
SLOTS = 8
N_PIPE = 8
N_DP = 32


def draw_slot_table(key, part):
    key = jax.random.fold_in(key, 11)
    order = jax.random.permutation(key, N_DP * SLOTS).astype(jnp.int32)
    return jnp.where(order < NBLK, order, -1).astype(jnp.int32)


def draw_row_counts(key, part):
    key = jax.random.fold_in(key, 12)
    count_key, first_key, second_key = jax.random.split(key, 3)
    devices_all = N_PIPE * N_DP
    counts = jax.random.randint(count_key, (devices_all,), TOK_DEV // 4, TOK_DEV + 1)
    first = jax.random.randint(first_key, (), 0, devices_all)
    second = (first + 1 + jax.random.randint(second_key, (), 0, devices_all - 1)) % devices_all
    places = jnp.arange(devices_all)
    counts = jnp.where(places == first, TOK_DEV, counts)
    counts = jnp.where(places == second, TOK_DEV // 4, counts)
    return counts.astype(jnp.int32)


def draw_acts(key, part):
    key = jax.random.fold_in(key, 13)
    noise_key, scale_key = jax.random.split(key)
    noise = jax.random.normal(noise_key, (TOKENS, D), jnp.float32)
    top = math.log(3.0)
    mixed = noise + 0.6 * jnp.roll(noise, -1, axis=1)
    scales = jnp.exp(jax.random.uniform(scale_key, (D,), jnp.float32, math.log(0.3), top))
    return (mixed * scales[None, :]).astype(jnp.bfloat16)


def draw_old_cov(key, part):
    key = jax.random.fold_in(key, 14)
    diag_key, off_key = jax.random.split(key)
    top = math.log(10.0)
    diag = jnp.exp(jax.random.uniform(diag_key, (N_DP, SLOTS, B), jnp.float32, 0.0, top))
    off = jax.random.uniform(off_key, (N_DP, SLOTS, B, B), jnp.float32, -1.0, 1.0) * (0.8 / B)
    off = 0.5 * (off + jnp.swapaxes(off, 2, 3))
    eye = jnp.eye(B, dtype=jnp.float32)
    return off * (1.0 - eye) + diag[..., None] * eye


def shard_levels(own_key, extent, shards, least, high):
    loudness = 1.0
    for axis_at, blocks in shards:
        steps = jax.random.uniform(jax.random.fold_in(jax.random.fold_in(own_key, 6), axis_at), (blocks,), jnp.float32, least / len(shards), high / len(shards))
        loudness = loudness * jnp.repeat(jnp.exp(steps), extent[axis_at] // blocks).reshape((-1,) + (1,) * (len(extent) - 1 - axis_at))
    return loudness


def bell_draw(key, extent, scale, reach, shards=(), held_as=jnp.bfloat16):
    result = jax.random.normal(key, extent, jnp.float32) * scale
    if len(shards) > 0:
        result = shard_levels(key, extent, shards, -0.22, 0.18) * result
    return jnp.clip(result, min=-reach, max=reach).astype(held_as)


def setup_inputs(seed: int = 0) -> dict:
    keys = jax.random.split(jax.random.key(seed), 7)
    acts = draw_acts(jax.random.fold_in(keys[6], 71), 0)
    grads_out = bell_draw(keys[1], (TOKENS, FF), 1.0, 6.0, ((0, 256),))
    weight_grad = bell_draw(keys[2], (D, FF), 1.0, 6.0, ((0, 8), (1, 32)))
    slot_table = draw_slot_table(jax.random.fold_in(keys[6], 71), 0)
    row_counts = draw_row_counts(jax.random.fold_in(keys[6], 71), 0)
    old_cov = draw_old_cov(jax.random.fold_in(keys[6], 71), 0)
    return dict(acts=acts, grads_out=grads_out, weight_grad=weight_grad, slot_table=slot_table, row_counts=row_counts, old_cov=old_cov)


def invert_blocks(cov):
    eye = jnp.eye(cov.shape[-1], dtype=cov.dtype)
    chol = jnp.linalg.cholesky(cov + 0.1 * eye)
    solve_one = lambda factor: jax.scipy.linalg.cho_solve((factor, True), eye)
    return jax.vmap(solve_one)(chol)

def reference(acts, grads_out, weight_grad, slot_table, row_counts, old_cov):
    rows = jnp.arange(TOKENS, dtype=jnp.int32)
    owner_dev = rows // TOK_DEV
    live = rows % TOK_DEV < jnp.take(row_counts, owner_dev)
    total = jnp.sum(row_counts).astype(jnp.float32)

    def one_slot(block):
        first = jnp.clip(block, 0, NA - 1).astype(jnp.int32) * B
        second = jnp.clip(block - NA, 0, NG - 1).astype(jnp.int32) * B
        from_acts = lax.dynamic_slice_in_dim(acts, first, B, 1)
        from_grads = lax.dynamic_slice_in_dim(grads_out, second, B, 1)
        cols = jnp.where(block < NA, from_acts, from_grads)
        cols = jnp.where(live[:, None] & (block >= 0), cols, jnp.zeros_like(cols))
        return jnp.dot(cols.T.astype(jnp.float32), cols.astype(jnp.float32), preferred_element_type=jnp.float32)
    gram = lax.map(one_slot, slot_table).reshape(N_DP, SLOTS, B, B)
    new_cov = 0.8 * old_cov + 0.2 * gram / total
    inverse = invert_blocks(new_cov.reshape(N_DP * SLOTS, B, B)).astype(jnp.bfloat16)
    slot_ids = jnp.arange(N_DP * SLOTS, dtype=jnp.int32)

    def locate(wanted):
        hits = slot_table[None, :] == wanted[:, None]
        return jnp.sum(jnp.where(hits, slot_ids[None, :], 0), axis=1).astype(jnp.int32)
    a_inv = jnp.take(inverse, locate(jnp.arange(NA, dtype=jnp.int32)), axis=0)
    g_inv = jnp.take(inverse, locate(NA + jnp.arange(NG, dtype=jnp.int32)), axis=0)
    left = jnp.einsum('ixy,iyc->ixc', a_inv.astype(jnp.float32), weight_grad.reshape(NA, B, FF).astype(jnp.float32))
    left = left.astype(jnp.bfloat16).reshape(D, NG, B)
    right = jnp.einsum('rjy,jyz->rjz', left.astype(jnp.float32), g_inv.astype(jnp.float32))
    return (right.reshape(D, FF).astype(jnp.bfloat16), new_cov)
```

```python
import functools

import jax
import jax.numpy as jnp
from jax import lax
from jax.experimental import pallas as pl
from jax.experimental.pallas import tpu as pltpu
from jax.sharding import Mesh, PartitionSpec as P

B = 128
H = B // 2
BF = jnp.bfloat16
F32 = jnp.float32
EXTRA = 16
VMEM_LIMIT = 50 * 1024 * 1024


def iota(shape, dim):
    return lax.broadcasted_iota(jnp.int32, shape, dim)


def pack(sym):
    top = sym[:H, :]
    low = pltpu.roll(sym[H:, :], H, 1)
    row, lane = iota((H, B), 0), iota((H, B), 1)
    half = jnp.where(lane < row, low, top)
    diag = jnp.sum(jnp.where(lane == row, low, 0.0), axis=0, keepdims=True)
    return half, diag


def unpack(half, diag):
    row, lane = iota((H, B), 0), iota((H, B), 1)
    upper = jnp.where(lane >= row, half, 0.0)
    lower = jnp.where(lane < row, half, 0.0)
    lower = jnp.where(lane == row, diag, lower)
    lower = pltpu.roll(lower, H, 1)
    part = jnp.concatenate((upper, lower), axis=0)
    brow, blane = iota((B, B), 0), iota((B, B), 1)
    return part + jnp.where(brow == blane, 0.0, part.T)


def invert(mat):
    rows = 8
    groups = [mat[g * rows : (g + 1) * rows, :] for g in range(B // rows)]
    lane, sub = iota((rows, B), 1), iota((rows, B), 0)
    for k in range(B):
        at, inside = k // rows, k % rows
        own = groups[at]
        scale = 1.0 / own[inside : inside + 1, k : k + 1]
        line = jnp.where(lane[:1] == k, scale, own[inside : inside + 1, :] * scale)
        line = jnp.broadcast_to(line, (rows, B))
        fresh = []
        for g in range(B // rows):
            col = jnp.broadcast_to(groups[g][:, k : k + 1], (rows, B))
            new = jnp.where(lane == k, 0.0, groups[g]) - col * line
            if g == at:
                new = jnp.where(sub == inside, line, new)
            fresh.append(new)
        groups = fresh
    return jnp.concatenate(groups, axis=0)


def gram_kernel(acts_steps, chunk, slot_ref, me_ref, acts_ref, grads_ref, own_ref, send_ref, diag_ref):
    step = pl.program_id(0)
    live = me_ref[0]
    core = me_ref[1]
    group_rows = own_ref.shape[0] // 16

    @pl.when(step == 0)
    def _():
        own_ref[...] = jnp.zeros_like(own_ref)
        send_ref[...] = jnp.zeros_like(send_ref)
        diag_ref[...] = jnp.zeros_like(diag_ref)

    def work(x_ref):
        x = x_ref[...]
        x = jnp.where(iota(x.shape, 0) < live, x, jnp.zeros_like(x))
        for b in range(chunk):
            xb = x[:, b * B : (b + 1) * B]
            gram = lax.dot_general(xb, xb, (((0,), (0,)), ((), ())), preferred_element_type=F32)
            half, diag = pack(gram)
            half = half.astype(BF)
            slot = slot_ref[step * chunk + b]
            owner, row = slot // 8, slot % 8
            other = (owner % 2) != core
            group = owner // 2
            at = pl.multiple_of(group * group_rows + row * H, 16)

            @pl.when(other)
            def _():
                send_ref[pl.ds(at, H), :] = half

            @pl.when(jnp.logical_not(other))
            def _():
                own_ref[pl.ds(at, H), :] = half

            diag_ref[pl.ds(other.astype(jnp.int32) * 128 + group * 8 + row, 1), :] = diag

    pl.when(step < acts_steps)(lambda: work(acts_ref))
    pl.when(step >= acts_steps)(lambda: work(grads_ref))

    @pl.when(step == pl.num_programs(0) - 1)
    def _():
        count = jnp.full((8, B), live, jnp.int32).astype(F32)
        for rel, ref in ((0, own_ref), (1, send_ref)):
            for group in range(16):
                rows = diag_ref[pl.ds(rel * 128 + group * 8, 8), :]
                ref[pl.ds(group * group_rows + 8 * H, EXTRA), :] = jnp.concatenate((rows, count), axis=0).astype(BF)


def grams(slot_of, me, acts, grads_out):
    chunk = 8
    width = chunk * B
    tok = acts.shape[0]
    acts_steps = acts.shape[1] // width
    grads_steps = grads_out.shape[1] // width
    group_rows = 8 * H + EXTRA
    out = jax.ShapeDtypeStruct((16 * group_rows, B), BF)
    whole = pl.BlockSpec((16 * group_rows, B), lambda i, *_: (0, 0))
    return pl.pallas_call(
        functools.partial(gram_kernel, acts_steps, chunk),
        out_shape=(out, out),
        grid_spec=pltpu.PrefetchScalarGridSpec(
            num_scalar_prefetch=2,
            grid=(acts_steps + grads_steps,),
            in_specs=[
                pl.BlockSpec((tok, width), lambda i, *_: (0, jnp.minimum(i, acts_steps - 1))),
                pl.BlockSpec((tok, width), lambda i, *_: (0, jnp.maximum(i - acts_steps, 0))),
            ],
            out_specs=[whole, whole],
            scratch_shapes=[pltpu.VMEM((256, B), F32)],
        ),
        compiler_params=pltpu.CompilerParams(vmem_limit_bytes=VMEM_LIMIT),
        name="grams",
    )(slot_of, me, acts, grads_out)


def section_kernel(parts_ref, out_ref):
    for row in range(8):
        total = parts_ref[0, row * H : (row + 1) * H, :].astype(F32)
        for g in range(1, 16):
            total += parts_ref[g, row * H : (row + 1) * H, :].astype(F32)
        out_ref[row, :H, :] = total.astype(BF)
    extra = parts_ref[0, 8 * H :, :].astype(F32)
    for g in range(1, 16):
        extra += parts_ref[g, 8 * H :, :].astype(F32)
    count = extra[8:, :]
    high = jnp.floor(count * (1.0 / 256.0))
    low = count - 256.0 * high
    sub = iota((8, B), 0)
    for row in range(8):
        first = jnp.where(sub == 0, jnp.broadcast_to(extra[row : row + 1, :], (8, B)), jnp.where(sub == 1, high, low))
        out_ref[row, H:, :] = jnp.concatenate((first, jnp.zeros_like(first)), axis=0).astype(BF)


def section_sum(parts):
    return pl.pallas_call(
        section_kernel,
        out_shape=jax.ShapeDtypeStruct((8, H + EXTRA, B), BF),
        compiler_params=pltpu.CompilerParams(vmem_limit_bytes=VMEM_LIMIT),
        name="section_sum",
    )(parts)


def inverse_kernel(parts_ref, old_ref, cov_ref, out_ref):
    half = parts_ref[0, :H, :].astype(F32)
    extra = parts_ref[0, H:, :].astype(F32)
    for s in range(1, 8):
        half += parts_ref[s, :H, :].astype(F32)
        extra += parts_ref[s, H:, :].astype(F32)
    total = extra[1:2, :] * 256.0 + extra[2:3, :]
    gram = unpack(half, extra[:1, :])
    cov = 0.8 * old_ref[0, 0] + 0.2 * gram / total
    cov_ref[0, 0] = cov
    eye = jnp.where(iota((B, B), 0) == iota((B, B), 1), 0.1, 0.0)
    inv_half, inv_diag = pack(invert(cov + eye))
    out_ref[:H, :] = inv_half.astype(BF)
    out_ref[H:, :] = jnp.broadcast_to(inv_diag, (EXTRA, B)).astype(BF)


def inverse(parts, old_cov):
    return pl.pallas_call(
        inverse_kernel,
        out_shape=(
            jax.ShapeDtypeStruct(old_cov.shape, F32),
            jax.ShapeDtypeStruct((H + EXTRA, B), BF),
        ),
        compiler_params=pltpu.CompilerParams(vmem_limit_bytes=VMEM_LIMIT),
        name="inverse",
    )(parts, old_cov)


def final_kernel(in_blocks, slot_ref, me_ref, inv_ref, weight_ref, out_ref, left_ref):
    section, owner = me_ref[2], me_ref[3]
    row_blocks = weight_ref.shape[0] // B
    col_blocks = weight_ref.shape[1] // B

    def block(which):
        slot = slot_ref[which]
        packed = inv_ref[slot].astype(F32)
        return unpack(packed[:H, :], packed[H : H + 1, :]).astype(BF)

    for i in range(row_blocks):
        rows = slice(i * B, (i + 1) * B)
        left = jnp.dot(block(section * row_blocks + i), weight_ref[rows, :], preferred_element_type=F32)
        left_ref[rows, :] = left.astype(BF)
    for j in range(col_blocks):
        cols = slice(j * B, (j + 1) * B)
        right = jnp.dot(left_ref[:, cols], block(in_blocks + owner * col_blocks + j), preferred_element_type=F32)
        out_ref[:, cols] = right.astype(BF)


def final(slot_of, me, inverses, weight_grad, in_blocks):
    smem = pl.BlockSpec(memory_space=pltpu.SMEM)
    vmem = pl.BlockSpec(memory_space=pltpu.VMEM)
    return pl.pallas_call(
        functools.partial(final_kernel, in_blocks),
        out_shape=jax.ShapeDtypeStruct(weight_grad.shape, BF),
        in_specs=[smem, smem, vmem, vmem],
        out_specs=vmem,
        scratch_shapes=[pltpu.VMEM(weight_grad.shape, BF)],
        compiler_params=pltpu.CompilerParams(vmem_limit_bytes=VMEM_LIMIT),
        name="final",
    )(slot_of, me, inverses, weight_grad)


def locate(slot_table, count):
    slot_ids = jnp.arange(slot_table.shape[0], dtype=jnp.int32)
    hits = slot_table[None, :] == jnp.arange(count, dtype=jnp.int32)[:, None]
    return jnp.sum(jnp.where(hits, slot_ids[None, :], 0), axis=1)


def on_device(acts, grads_out, weight_grad, slot_table, row_counts, old_cov):
    in_blocks = acts.shape[1] // B
    out_blocks = grads_out.shape[1] // B
    core = lax.axis_index("c")
    section = lax.axis_index("z")
    owner = (lax.axis_index("y") * 4 + lax.axis_index("x")) * 2 + core
    slot_of = locate(slot_table, in_blocks + out_blocks)
    me = jnp.stack((row_counts[0], core, section, owner)).astype(jnp.int32)
    own, send = grams(slot_of, me, acts, grads_out)
    got = lax.ppermute(send, "c", [(0, 1), (1, 0)])
    chip = (own.astype(F32) + got.astype(F32)).astype(BF)
    chip = chip.reshape(16, -1, B)
    plane = lax.all_to_all(chip, ("y", "x"), split_axis=0, concat_axis=0, tiled=True)
    share = lax.all_to_all(section_sum(plane), "z", split_axis=0, concat_axis=0, tiled=True)
    new_cov, inv = inverse(share, old_cov)
    column = lax.all_gather(inv, "z", axis=0)
    inverses = lax.all_gather(column, ("y", "x", "c"), axis=0, tiled=True)
    return final(slot_of, me, inverses, weight_grad, in_blocks), new_cov


def solution(mesh):
    wide = Mesh(mesh.devices.reshape(8, 4, 4, 2), ("z", "y", "x", "c"))
    dp = ("y", "x", "c")
    in_specs = (
        P(("z",) + dp, None),
        P(("z",) + dp, None),
        P("z", dp),
        P(),
        P(("z",) + dp),
        P(dp, "z", None, None),
    )
    out_specs = (P("z", dp), P(dp, "z", None, None))
    return jax.shard_map(
        on_device, mesh=wide, in_specs=in_specs, out_specs=out_specs, check_vma=False
    )
```

```python
import functools

import jax
import jax.numpy as jnp
from jax import lax
from jax.experimental import pallas as pl
from jax.experimental.pallas import tpu as pltpu
from jax.sharding import Mesh, PartitionSpec as P

B = 128
H = B // 2
BF = jnp.bfloat16
F32 = jnp.float32
EXTRA = 16
VMEM_LIMIT = 24 * 1024 * 1024


def iota(shape, dim):
    return lax.broadcasted_iota(jnp.int32, shape, dim)


def pack(sym):
    top = sym[:H, :]
    low = pltpu.roll(sym[H:, :], H, 1)
    row, lane = iota((H, B), 0), iota((H, B), 1)
    half = jnp.where(lane < row, low, top)
    diag = jnp.sum(jnp.where(lane == row, low, 0.0), axis=0, keepdims=True)
    return half, diag


def unpack(half, diag):
    row, lane = iota((H, B), 0), iota((H, B), 1)
    upper = jnp.where(lane >= row, half, 0.0)
    lower = jnp.where(lane < row, half, 0.0)
    lower = jnp.where(lane == row, diag, lower)
    lower = pltpu.roll(lower, H, 1)
    part = jnp.concatenate((upper, lower), axis=0)
    brow, blane = iota((B, B), 0), iota((B, B), 1)
    return part + jnp.where(brow == blane, 0.0, part.T)


def invert(mat):
    rows = 8
    groups = [mat[g * rows : (g + 1) * rows, :] for g in range(B // rows)]
    lane, sub = iota((rows, B), 1), iota((rows, B), 0)
    for k in range(B):
        at, inside = k // rows, k % rows
        own = groups[at]
        scale = 1.0 / own[inside : inside + 1, k : k + 1]
        line = jnp.where(lane[:1] == k, scale, own[inside : inside + 1, :] * scale)
        line = jnp.broadcast_to(line, (rows, B))
        fresh = []
        for g in range(B // rows):
            col = jnp.broadcast_to(groups[g][:, k : k + 1], (rows, B))
            new = jnp.where(lane == k, 0.0, groups[g]) - col * line
            if g == at:
                new = jnp.where(sub == inside, line, new)
            fresh.append(new)
        groups = fresh
    return jnp.concatenate(groups, axis=0)


def gram_kernel(away, table_ref, me_ref, acts_ref, grads_ref, out_ref):
    live, core = me_ref[0], me_ref[1]
    want = 1 - core if away else core
    in_blocks = acts_ref.shape[1] // B
    out_blocks = grads_ref.shape[1] // B
    group_rows = 8 * H + EXTRA
    unroll = 2

    @pl.loop(0, 16 // unroll)
    def _(trip):
        for inner in range(unroll):
            group = trip * unroll + inner
            base = pl.multiple_of(group * group_rows, 16)
            diags = jnp.zeros((8, B), F32)
            for row in range(8):
                which = table_ref[(group * 2 + want) * 8 + row]
                filled = jnp.where(which >= 0, live, 0)
                first = pl.multiple_of(jnp.clip(which, 0, in_blocks - 1) * B, B)
                second = pl.multiple_of(jnp.clip(which - in_blocks, 0, out_blocks - 1) * B, B)
                x = jnp.where(which < in_blocks, acts_ref[:, pl.ds(first, B)], grads_ref[:, pl.ds(second, B)])
                x = jnp.where(iota(x.shape, 0) < filled, x, jnp.zeros_like(x))
                gram = lax.dot_general(x, x, (((0,), (0,)), ((), ())), preferred_element_type=F32)
                half, diag = pack(gram)
                out_ref[pl.ds(base + row * H, H), :] = half.astype(BF)
                diags = jnp.where(iota((8, B), 0) == row, diag, diags)
            count = jnp.full((8, B), live, jnp.int32).astype(F32)
            out_ref[pl.ds(base + 8 * H, EXTRA), :] = jnp.concatenate((diags, count), axis=0).astype(BF)


def grams(away, table, me, acts, grads_out):
    smem = pl.BlockSpec(memory_space=pltpu.SMEM)
    vmem = pl.BlockSpec(memory_space=pltpu.VMEM)
    return pl.pallas_call(
        functools.partial(gram_kernel, away),
        out_shape=jax.ShapeDtypeStruct((16 * (8 * H + EXTRA), B), BF),
        in_specs=[smem, smem, vmem, vmem],
        out_specs=vmem,
        compiler_params=pltpu.CompilerParams(vmem_limit_bytes=VMEM_LIMIT),
        cost_estimate=pl.CostEstimate(flops=2 * 128 * B**3, bytes_accessed=16 * 2**20, transcendentals=0),
        name="grams_away" if away else "grams_own",
    )(table, me, acts, grads_out)


def section_kernel(parts_ref, out_ref):
    for row in range(8):
        total = parts_ref[0, row * H : (row + 1) * H, :].astype(F32)
        for g in range(1, 16):
            total += parts_ref[g, row * H : (row + 1) * H, :].astype(F32)
        out_ref[row, :H, :] = total.astype(BF)
    extra = parts_ref[0, 8 * H :, :].astype(F32)
    for g in range(1, 16):
        extra += parts_ref[g, 8 * H :, :].astype(F32)
    count = extra[8:, :]
    high = jnp.floor(count * (1.0 / 256.0))
    low = count - 256.0 * high
    sub = iota((8, B), 0)
    for row in range(8):
        first = jnp.where(sub == 0, jnp.broadcast_to(extra[row : row + 1, :], (8, B)), jnp.where(sub == 1, high, low))
        out_ref[row, H:, :] = jnp.concatenate((first, jnp.zeros_like(first)), axis=0).astype(BF)


def section_sum(parts):
    return pl.pallas_call(
        section_kernel,
        out_shape=jax.ShapeDtypeStruct((8, H + EXTRA, B), BF),
        compiler_params=pltpu.CompilerParams(vmem_limit_bytes=VMEM_LIMIT),
        name="section_sum",
    )(parts)


def inverse_kernel(parts_ref, old_ref, cov_ref, out_ref):
    half = parts_ref[0, :H, :].astype(F32)
    extra = parts_ref[0, H:, :].astype(F32)
    for s in range(1, 8):
        half += parts_ref[s, :H, :].astype(F32)
        extra += parts_ref[s, H:, :].astype(F32)
    total = extra[1:2, :] * 256.0 + extra[2:3, :]
    gram = unpack(half, extra[:1, :])
    cov = 0.8 * old_ref[0, 0] + 0.2 * gram / total
    cov_ref[0, 0] = cov
    eye = jnp.where(iota((B, B), 0) == iota((B, B), 1), 0.1, 0.0)
    inv_half, inv_diag = pack(invert(cov + eye))
    packed = jnp.concatenate((inv_half, jnp.broadcast_to(inv_diag, (EXTRA, B))), axis=0).astype(BF)
    for g in range(16):
        out_ref[g] = packed


def inverse(parts, old_cov):
    return pl.pallas_call(
        inverse_kernel,
        out_shape=(
            jax.ShapeDtypeStruct(old_cov.shape, F32),
            jax.ShapeDtypeStruct((16, H + EXTRA, B), BF),
        ),
        compiler_params=pltpu.CompilerParams(vmem_limit_bytes=VMEM_LIMIT),
        name="inverse",
    )(parts, old_cov)


def route_kernel(in_blocks, row_blocks, col_blocks, slot_ref, me_ref, mine_ref, other_ref, out_ref):
    core, owner = me_ref[1], me_ref[3]
    share = row_blocks // 2
    sub = iota((EXTRA, B), 0)

    def packed(which):
        holder = slot_ref[which] // 8
        same = (holder % 2) == core
        return jnp.where(same, mine_ref[holder // 2], other_ref[holder // 2])

    cols = []
    col_diags = jnp.zeros((EXTRA, B), F32)
    for j in range(col_blocks):
        block = packed(in_blocks + owner * col_blocks + j)
        cols.append(block[:H, :])
        col_diags = jnp.where(sub == j, block[H:, :].astype(F32), col_diags)
    for section in range(8):
        diags = col_diags
        for j in range(col_blocks):
            out_ref[section, j * H : (j + 1) * H, :] = cols[j]
        for i in range(share):
            block = packed(section * row_blocks + core * share + i)
            at = (col_blocks + i) * H
            out_ref[section, at : at + H, :] = block[:H, :]
            diags = jnp.where(sub == col_blocks + i, block[H:, :].astype(F32), diags)
        out_ref[section, (col_blocks + share) * H :, :] = diags.astype(BF)


def route(slot_of, me, mine, other, in_blocks, row_blocks, col_blocks):
    smem = pl.BlockSpec(memory_space=pltpu.SMEM)
    vmem = pl.BlockSpec(memory_space=pltpu.VMEM)
    rows = (col_blocks + row_blocks // 2) * H + EXTRA
    return pl.pallas_call(
        functools.partial(route_kernel, in_blocks, row_blocks, col_blocks),
        out_shape=jax.ShapeDtypeStruct((8, rows, B), BF),
        in_specs=[smem, smem, vmem, vmem],
        out_specs=vmem,
        compiler_params=pltpu.CompilerParams(vmem_limit_bytes=VMEM_LIMIT),
        name="route",
    )(slot_of, me, mine, other)


def pick_kernel(row_blocks, col_blocks, slot_ref, me_ref, got_ref, out_ref):
    core, section = me_ref[1], me_ref[2]
    share = row_blocks // 2
    sub = iota((EXTRA, B), 0)
    for i in range(share):
        source = slot_ref[section * row_blocks + core * share + i] % 8
        at = (col_blocks + i) * H
        out_ref[i, :H, :] = got_ref[source, at : at + H, :]
        diags = got_ref[source, (col_blocks + share) * H :, :].astype(F32)
        diag = jnp.sum(jnp.where(sub == col_blocks + i, diags, 0.0), axis=0, keepdims=True)
        out_ref[i, H:, :] = jnp.broadcast_to(diag, (EXTRA, B)).astype(BF)


def pick(slot_of, me, got, row_blocks, col_blocks):
    smem = pl.BlockSpec(memory_space=pltpu.SMEM)
    vmem = pl.BlockSpec(memory_space=pltpu.VMEM)
    return pl.pallas_call(
        functools.partial(pick_kernel, row_blocks, col_blocks),
        out_shape=jax.ShapeDtypeStruct((row_blocks // 2, H + EXTRA, B), BF),
        in_specs=[smem, smem, vmem],
        out_specs=vmem,
        compiler_params=pltpu.CompilerParams(vmem_limit_bytes=VMEM_LIMIT),
        name="pick",
    )(slot_of, me, got)


def final_kernel(in_blocks, slot_ref, me_ref, got_ref, mine_ref, other_ref, weight_ref, out_ref, left_ref):
    core, owner = me_ref[1], me_ref[3]
    row_blocks = weight_ref.shape[0] // B
    col_blocks = weight_ref.shape[1] // B
    share = row_blocks // 2
    sub = iota((EXTRA, B), 0)
    for i in range(row_blocks):
        same = core == i // share
        packed = jnp.where(same, mine_ref[i % share], other_ref[i % share]).astype(F32)
        block = unpack(packed[:H, :], packed[H : H + 1, :]).astype(BF)
        rows = slice(i * B, (i + 1) * B)
        left = jnp.dot(block, weight_ref[rows, :], preferred_element_type=F32)
        left_ref[rows, :] = left.astype(BF)
    for j in range(col_blocks):
        source = slot_ref[in_blocks + owner * col_blocks + j] % 8
        half = got_ref[source, j * H : (j + 1) * H, :].astype(F32)
        diags = got_ref[source, (col_blocks + share) * H :, :].astype(F32)
        diag = jnp.sum(jnp.where(sub == j, diags, 0.0), axis=0, keepdims=True)
        block = unpack(half, diag).astype(BF)
        cols = slice(j * B, (j + 1) * B)
        right = jnp.dot(left_ref[:, cols], block, preferred_element_type=F32)
        out_ref[:, cols] = right.astype(BF)


def final(slot_of, me, got, mine, other, weight_grad, in_blocks):
    smem = pl.BlockSpec(memory_space=pltpu.SMEM)
    vmem = pl.BlockSpec(memory_space=pltpu.VMEM)
    return pl.pallas_call(
        functools.partial(final_kernel, in_blocks),
        out_shape=jax.ShapeDtypeStruct(weight_grad.shape, BF),
        in_specs=[smem, smem, vmem, vmem, vmem, vmem],
        out_specs=vmem,
        scratch_shapes=[pltpu.VMEM(weight_grad.shape, BF)],
        compiler_params=pltpu.CompilerParams(vmem_limit_bytes=VMEM_LIMIT),
        name="final",
    )(slot_of, me, got, mine, other, weight_grad)


def locate(slot_table, count):
    slot_ids = jnp.arange(slot_table.shape[0], dtype=jnp.int32)
    hits = slot_table[None, :] == jnp.arange(count, dtype=jnp.int32)[:, None]
    return jnp.sum(jnp.where(hits, slot_ids[None, :], 0), axis=1)


def on_device(acts, grads_out, weight_grad, slot_table, row_counts, old_cov):
    in_blocks = acts.shape[1] // B
    out_blocks = grads_out.shape[1] // B
    core = lax.axis_index("c")
    section = lax.axis_index("z")
    owner = (lax.axis_index("y") * 4 + lax.axis_index("x")) * 2 + core
    slot_of = locate(slot_table, in_blocks + out_blocks)
    me = jnp.stack((row_counts[0], core, section, owner)).astype(jnp.int32)
    swap = [(0, 1), (1, 0)]
    away = grams(True, slot_table, me, acts, grads_out)
    got = lax.ppermute(away, "c", swap)
    own = grams(False, slot_table, me, acts, grads_out)
    chip = (own.astype(F32) + got.astype(F32)).astype(BF)
    chip = chip.reshape(16, -1, B)
    plane = lax.all_to_all(chip, ("y", "x"), split_axis=0, concat_axis=0, tiled=True)
    share = lax.all_to_all(section_sum(plane), "z", split_axis=0, concat_axis=0, tiled=True)
    new_cov, inv = inverse(share, old_cov)
    mine = lax.all_to_all(inv, ("y", "x"), split_axis=0, concat_axis=0, tiled=True)
    other = lax.ppermute(mine, "c", swap)
    row_blocks = weight_grad.shape[0] // B
    col_blocks = weight_grad.shape[1] // B
    routed = route(slot_of, me, mine, other, in_blocks, row_blocks, col_blocks)
    got = lax.all_to_all(routed, "z", split_axis=0, concat_axis=0, tiled=True)
    mine = pick(slot_of, me, got, row_blocks, col_blocks)
    other = lax.ppermute(mine, "c", swap)
    return final(slot_of, me, got, mine, other, weight_grad, in_blocks), new_cov


def solution(mesh):
    wide = Mesh(mesh.devices.reshape(8, 4, 4, 2), ("z", "y", "x", "c"))
    dp = ("y", "x", "c")
    in_specs = (
        P(("z",) + dp, None),
        P(("z",) + dp, None),
        P("z", dp),
        P(),
        P(("z",) + dp),
        P(dp, "z", None, None),
    )
    out_specs = (P("z", dp), P(dp, "z", None, None))
    return jax.shard_map(
        on_device, mesh=wide, in_specs=in_specs, out_specs=out_specs, check_vma=False
    )
```

```python
import functools

import jax
import jax.numpy as jnp
import numpy as np
from jax import lax
from jax.experimental import pallas as pl
from jax.experimental.pallas import tpu as pltpu
from jax.sharding import Mesh, PartitionSpec as P

B = 128
H = B // 2
BF = jnp.bfloat16
F32 = jnp.float32
EXTRA = 16
VMEM_LIMIT = 24 * 1024 * 1024


def iota(shape, dim):
    return lax.broadcasted_iota(jnp.int32, shape, dim)


def pack(sym):
    top = sym[:H, :]
    low = pltpu.roll(sym[H:, :], H, 1)
    row, lane = iota((H, B), 0), iota((H, B), 1)
    half = jnp.where(lane < row, low, top)
    diag = jnp.sum(jnp.where(lane == row, low, 0.0), axis=0, keepdims=True)
    return half, diag


def unpack(half, diag):
    row, lane = iota((H, B), 0), iota((H, B), 1)
    upper = jnp.where(lane >= row, half, 0.0)
    lower = jnp.where(lane < row, half, 0.0)
    lower = jnp.where(lane == row, diag, lower)
    lower = pltpu.roll(lower, H, 1)
    part = jnp.concatenate((upper, lower), axis=0)
    brow, blane = iota((B, B), 0), iota((B, B), 1)
    return part + jnp.where(brow == blane, 0.0, part.T)


def eliminate(groups, k, m, solve):
    rows = 8
    lane, sub = iota((rows, B), 1), iota((rows, B), 0)
    at, inside = k // rows, k % rows
    spread = lambda v: jnp.broadcast_to(v, (rows, B))
    cols = [[spread(g[:, k + i : k + i + 1]) for g in groups] for i in range(m)]
    pivot = [[spread(cols[j][at][inside + i : inside + i + 1, :]) for j in range(m)] for i in range(m)]
    inv = solve(pivot)
    lines = [spread(groups[at][inside + i : inside + i + 1, :]) for i in range(m)]
    fresh_lines = []
    for i in range(m):
        line = inv[i][0] * lines[0]
        for j in range(1, m):
            line = line + inv[i][j] * lines[j]
        for j in range(m):
            line = jnp.where(lane == k + j, inv[i][j], line)
        fresh_lines.append(line)
    out = []
    inner = (lane >= k) & (lane < k + m)
    for g in range(B // rows):
        new = jnp.where(inner, 0.0, groups[g])
        for i in range(m):
            new = new - cols[i][g] * fresh_lines[i]
        if g == at:
            for i in range(m):
                new = jnp.where(sub == inside + i, fresh_lines[i], new)
        out.append(new)
    return out


def solve2(p):
    a, b, c = p[0][0], p[0][1], p[1][1]
    scale = 1.0 / (a * c - b * b)
    off = -b * scale
    return [[c * scale, off], [off, a * scale]]


def solve4(p):
    e = solve2([p[0][:2], p[1][:2]])
    f = [row[2:] for row in p[:2]]
    m = [[e[i][0] * f[0][j] + e[i][1] * f[1][j] for j in range(2)] for i in range(2)]
    s = [[p[2 + i][2 + j] - (f[0][i] * m[0][j] + f[1][i] * m[1][j]) for j in range(2)] for i in range(2)]
    si = solve2(s)
    x = [[m[i][0] * si[0][j] + m[i][1] * si[1][j] for j in range(2)] for i in range(2)]
    top = [[e[i][j] + x[i][0] * m[j][0] + x[i][1] * m[j][1] for j in range(2)] + [-x[i][0], -x[i][1]] for i in range(2)]
    low = [[-x[0][i], -x[1][i]] + si[i] for i in range(2)]
    return top + low


def invert(mat):
    groups = [mat[g * 8 : (g + 1) * 8, :] for g in range(B // 8)]
    for k in range(0, B, 4):
        groups = eliminate(groups, k, 4, solve4)
    return jnp.concatenate(groups, axis=0)


def gram_kernel(away, table_ref, me_ref, acts_ref, grads_ref, out_ref):
    live, core = me_ref[0], me_ref[1]
    want = 1 - core if away else core
    in_blocks = acts_ref.shape[1] // B
    out_blocks = grads_ref.shape[1] // B
    group_rows = 8 * H + EXTRA
    unroll = 2

    @pl.loop(0, 16 // unroll)
    def _(trip):
        for inner in range(unroll):
            group = trip * unroll + inner
            base = pl.multiple_of(group * group_rows, 16)
            diags = jnp.zeros((8, B), F32)
            for row in range(8):
                which = table_ref[(group * 2 + want) * 8 + row]
                filled = jnp.where(which >= 0, live, 0)
                first = pl.multiple_of(jnp.clip(which, 0, in_blocks - 1) * B, B)
                second = pl.multiple_of(jnp.clip(which - in_blocks, 0, out_blocks - 1) * B, B)
                x = jnp.where(which < in_blocks, acts_ref[:, pl.ds(first, B)], grads_ref[:, pl.ds(second, B)])
                x = jnp.where(iota(x.shape, 0) < filled, x, jnp.zeros_like(x))
                gram = lax.dot_general(x, x, (((0,), (0,)), ((), ())), preferred_element_type=F32)
                half, diag = pack(gram)
                out_ref[pl.ds(base + row * H, H), :] = half.astype(BF)
                diags = jnp.where(iota((8, B), 0) == row, diag, diags)
            count = jnp.full((8, B), live, jnp.int32).astype(F32)
            out_ref[pl.ds(base + 8 * H, EXTRA), :] = jnp.concatenate((diags, count), axis=0).astype(BF)


def grams(away, table, me, acts, grads_out):
    smem = pl.BlockSpec(memory_space=pltpu.SMEM)
    vmem = pl.BlockSpec(memory_space=pltpu.VMEM)
    return pl.pallas_call(
        functools.partial(gram_kernel, away),
        out_shape=jax.ShapeDtypeStruct((16 * (8 * H + EXTRA), B), BF),
        in_specs=[smem, smem, vmem, vmem],
        out_specs=vmem,
        compiler_params=pltpu.CompilerParams(vmem_limit_bytes=VMEM_LIMIT),
        cost_estimate=pl.CostEstimate(flops=2 * 128 * B**3, bytes_accessed=16 * 2**20, transcendentals=0),
        name="grams_away" if away else "grams_own",
    )(table, me, acts, grads_out)


def home_table():
    table = np.full((16, 2, 8), -1, np.int32)
    for chip in range(16):
        y, x = divmod(chip, 4)
        for core in range(2):
            at = 48 + 6 * (chip * 2 + core)
            for section in range(8):
                if section % 4 != x:
                    table[chip, core, section] = at
                    at += 1
                elif y < 3:
                    table[chip, core, section] = 6 * section + 2 * y + core
    return table.reshape(-1)


def home_of(table, count):
    places = np.zeros((count,), np.int32)
    for place, block in enumerate(table):
        if block >= 0:
            places[block] = place
    return places


SMEM = pl.BlockSpec(memory_space=pltpu.SMEM)
VMEM = pl.BlockSpec(memory_space=pltpu.VMEM)
PARAMS = pltpu.CompilerParams(vmem_limit_bytes=VMEM_LIMIT)


def take_row(rows, at):
    return jnp.sum(jnp.where(iota((EXTRA, B), 0) == at, rows, 0.0), axis=0, keepdims=True)


def stack_rows(rows):
    out = jnp.zeros((EXTRA, B), F32)
    for at, row in enumerate(rows):
        out = jnp.where(iota((EXTRA, B), 0) == at, jnp.broadcast_to(row, (EXTRA, B)), out)
    return out


def split(value):
    high = value.astype(BF).astype(F32)
    return high, value - high


def section_kernel(home_ref, slot_ref, me_ref, parts_ref, old_ref, out_ref):
    owner = me_ref[3]
    extra = parts_ref[0, 8 * H :, :].astype(F32)
    for g in range(1, 16):
        extra += parts_ref[g, 8 * H :, :].astype(F32)
    count = extra[8:9, :]
    count_high = jnp.floor(count * (1.0 / 256.0))
    count_low = count - 256.0 * count_high
    for row in range(8):
        total = parts_ref[0, row * H : (row + 1) * H, :].astype(F32)
        for g in range(1, 16):
            total += parts_ref[g, row * H : (row + 1) * H, :].astype(F32)
        out_ref[row, :H, :] = total.astype(BF)
        block = jnp.maximum(home_ref[owner * 8 + row], 0)
        old_half, old_diag = pack(old_ref[slot_ref[block] // 8])
        high, low = split(old_half)
        out_ref[row, H : 2 * H, :] = high.astype(BF)
        out_ref[row, 2 * H : 3 * H, :] = low.astype(BF)
        high, low = split(old_diag)
        out_ref[row, 3 * H :, :] = stack_rows((extra[row : row + 1, :], count_high, count_low, high, low)).astype(BF)


def section_sum(home, slot_of, me, parts, old_row):
    return pl.pallas_call(
        section_kernel,
        out_shape=jax.ShapeDtypeStruct((8, 3 * H + EXTRA, B), BF),
        in_specs=[SMEM, SMEM, SMEM, VMEM, VMEM],
        out_specs=VMEM,
        compiler_params=PARAMS,
        name="section_sum",
    )(home, slot_of, me, parts, old_row)


def inverse_kernel(home_ref, slot_ref, me_ref, parts_ref, out_ref):
    section, owner = me_ref[2], me_ref[3]
    block = jnp.maximum(home_ref[owner * 8 + section], 0)
    source = slot_ref[block] % 8
    half = parts_ref[0, :H, :].astype(F32)
    extra = parts_ref[0, 3 * H :, :].astype(F32)
    for s in range(1, 8):
        half += parts_ref[s, :H, :].astype(F32)
        extra += parts_ref[s, 3 * H :, :].astype(F32)
    total = extra[1:2, :] * 256.0 + extra[2:3, :]
    gram_half = 0.2 * half / total
    gram_diag = 0.2 * extra[:1, :] / total
    old_half = parts_ref[source, H : 2 * H, :].astype(F32) + parts_ref[source, 2 * H : 3 * H, :].astype(F32)
    old_extra = parts_ref[source, 3 * H :, :].astype(F32)
    cov = unpack(0.8 * old_half + gram_half, 0.8 * (old_extra[3:4, :] + old_extra[4:5, :]) + gram_diag)
    eye = jnp.where(iota((B, B), 0) == iota((B, B), 1), 0.1, 0.0)
    inv_half, inv_diag = pack(invert(cov + eye))
    packed = jnp.concatenate((inv_half, gram_half, stack_rows((inv_diag, gram_diag))), axis=0).astype(BF)
    for s in range(8):
        out_ref[s] = packed


def inverse(home, slot_of, me, parts):
    return pl.pallas_call(
        inverse_kernel,
        out_shape=jax.ShapeDtypeStruct((8, 2 * H + EXTRA, B), BF),
        in_specs=[SMEM, SMEM, SMEM, VMEM],
        out_specs=VMEM,
        compiler_params=PARAMS,
        name="inverse",
    )(home, slot_of, me, parts)


def route_kernel(table_ref, place_ref, me_ref, mine_ref, other_ref, out_ref):
    core, section = me_ref[1], me_ref[2]
    halves, diags = [], []
    for c in range(2):
        packed = jnp.where(core == c, mine_ref[section], other_ref[section])
        halves.append(packed[:H, :])
        diags.append(take_row(packed[2 * H :, :].astype(F32), 0))
    for chip in range(16):
        block = jnp.maximum(table_ref[(chip * 2 + core) * 8 + section], 0)
        place = place_ref[block]
        same = (place // 8) % 2 == core
        at = place % 8
        half = jnp.where(same, mine_ref[at, H : 2 * H, :], other_ref[at, H : 2 * H, :])
        extra = jnp.where(same, mine_ref[at, 2 * H :, :], other_ref[at, 2 * H :, :]).astype(F32)
        out_ref[chip, :H, :] = halves[0]
        out_ref[chip, H : 2 * H, :] = halves[1]
        out_ref[chip, 2 * H : 3 * H, :] = half
        out_ref[chip, 3 * H :, :] = stack_rows((diags[0], diags[1], take_row(extra, 1))).astype(BF)


def route(table, places, me, mine, other):
    return pl.pallas_call(
        route_kernel,
        out_shape=jax.ShapeDtypeStruct((16, 3 * H + EXTRA, B), BF),
        in_specs=[SMEM, SMEM, SMEM, VMEM, VMEM],
        out_specs=VMEM,
        compiler_params=PARAMS,
        name="route",
    )(table, places, me, mine, other)


def final_kernel(table_ref, place_ref, me_ref, plane_ref, column_ref, old_ref, weight_ref, out_ref, cov_ref, left_ref):
    section, owner = me_ref[2], me_ref[3]
    row_blocks = weight_ref.shape[0] // B
    col_blocks = weight_ref.shape[1] // B
    for i in range(row_blocks):
        chip = i // 2 * 4 + section % 4
        half = plane_ref[chip, i % 2 * H : (i % 2 + 1) * H, :].astype(F32)
        diag = take_row(plane_ref[chip, 3 * H :, :].astype(F32), i % 2)
        rows = slice(i * B, (i + 1) * B)
        left = jnp.dot(unpack(half, diag).astype(BF), weight_ref[rows, :], preferred_element_type=F32)
        left_ref[rows, :] = left.astype(BF)
    skipped = (owner // 2) % 4
    for j in range(col_blocks):
        turn, at = j // 3 * 4, j % 3
        home = turn + at + jnp.where(skipped <= at, 1, 0)
        half = column_ref[home, :H, :].astype(F32)
        diag = take_row(column_ref[home, 2 * H :, :].astype(F32), 0)
        cols = slice(j * B, (j + 1) * B)
        right = jnp.dot(left_ref[:, cols], unpack(half, diag).astype(BF), preferred_element_type=F32)
        out_ref[:, cols] = right.astype(BF)
    block = table_ref[owner * 8 + section]
    chip = place_ref[jnp.maximum(block, 0)] // 16
    half = plane_ref[chip, 2 * H : 3 * H, :].astype(F32)
    diag = take_row(plane_ref[chip, 3 * H :, :].astype(F32), 2)
    cov_ref[0, 0] = 0.8 * old_ref[0, 0] + jnp.where(block >= 0, unpack(half, diag), 0.0)


def final(table, places, me, plane, column, old_cov, weight_grad):
    return pl.pallas_call(
        final_kernel,
        out_shape=(
            jax.ShapeDtypeStruct(weight_grad.shape, BF),
            jax.ShapeDtypeStruct(old_cov.shape, F32),
        ),
        in_specs=[SMEM, SMEM, SMEM, VMEM, VMEM, VMEM, VMEM],
        out_specs=(VMEM, VMEM),
        scratch_shapes=[pltpu.VMEM(weight_grad.shape, BF)],
        compiler_params=PARAMS,
        name="final",
    )(table, places, me, plane, column, old_cov, weight_grad)


def locate(slot_table, count):
    slot_ids = jnp.arange(slot_table.shape[0], dtype=jnp.int32)
    hits = slot_table[None, :] == jnp.arange(count, dtype=jnp.int32)[:, None]
    return jnp.sum(jnp.where(hits, slot_ids[None, :], 0), axis=1)


def on_device(acts, grads_out, weight_grad, slot_table, row_counts, old_cov):
    blocks = (acts.shape[1] + grads_out.shape[1]) // B
    plane, swap = ("y", "x"), [(0, 1), (1, 0)]
    exchange = functools.partial(lax.all_to_all, split_axis=0, concat_axis=0, tiled=True)
    old_row = lax.all_gather(old_cov[0, 0], plane + ("c",), axis=0)
    core = lax.axis_index("c")
    section = lax.axis_index("z")
    owner = (lax.axis_index("y") * 4 + lax.axis_index("x")) * 2 + core
    me = jnp.stack((row_counts[0], core, section, owner)).astype(jnp.int32)
    table = home_table()
    home, places = jnp.asarray(table), jnp.asarray(home_of(table, blocks))
    slot_of = locate(slot_table, blocks)
    away = grams(True, home, me, acts, grads_out)
    got = lax.ppermute(away, "c", swap)
    own = grams(False, home, me, acts, grads_out)
    chip = (own.astype(F32) + got.astype(F32)).astype(BF)
    parts = exchange(chip.reshape(16, -1, B), plane)
    share = exchange(section_sum(home, slot_of, me, parts, old_row), "z")
    mine = exchange(inverse(home, slot_of, me, share), "z")
    other = lax.ppermute(mine, "c", swap)
    row = exchange(route(slot_table, places, me, mine, other), plane)
    return final(slot_table, places, me, row, mine, old_cov, weight_grad)


def solution(mesh):
    wide = Mesh(mesh.devices.reshape(8, 4, 4, 2), ("z", "y", "x", "c"))
    dp = ("y", "x", "c")
    in_specs = (
        P(("z",) + dp, None),
        P(("z",) + dp, None),
        P("z", dp),
        P(),
        P(("z",) + dp),
        P(dp, "z", None, None),
    )
    out_specs = (P("z", dp), P(dp, "z", None, None))
    return jax.shard_map(
        on_device, mesh=wide, in_specs=in_specs, out_specs=out_specs, check_vma=False
    )
```

```python
import functools

import jax
import jax.numpy as jnp
import numpy as np
from jax import lax
from jax.experimental import pallas as pl
from jax.experimental.pallas import tpu as pltpu
from jax.sharding import Mesh, PartitionSpec as P

B = 128
H = B // 2
BF = jnp.bfloat16
F32 = jnp.float32
EXTRA = 16
ROOMS = (3, 4)
VMEM_LIMIT = 24 * 1024 * 1024


SMEM = pl.BlockSpec(memory_space=pltpu.SMEM)
VMEM = pl.BlockSpec(memory_space=pltpu.VMEM)
HBM = pl.BlockSpec(memory_space=pltpu.HBM)
PARAMS = pltpu.CompilerParams(vmem_limit_bytes=VMEM_LIMIT)


def iota(shape, dim):
    return lax.broadcasted_iota(jnp.int32, shape, dim)


def pack(sym):
    top = sym[:H, :]
    low = pltpu.roll(sym[H:, :], H, 1)
    row, lane = iota((H, B), 0), iota((H, B), 1)
    half = jnp.where(lane < row, low, top)
    diag = jnp.sum(jnp.where(lane == row, low, 0.0), axis=0, keepdims=True)
    return half, diag


def unpack(half, diag):
    row, lane = iota((H, B), 0), iota((H, B), 1)
    upper = jnp.where(lane >= row, half, 0.0)
    lower = jnp.where(lane < row, half, 0.0)
    lower = jnp.where(lane == row, diag, lower)
    lower = pltpu.roll(lower, H, 1)
    part = jnp.concatenate((upper, lower), axis=0)
    brow, blane = iota((B, B), 0), iota((B, B), 1)
    return part + jnp.where(brow == blane, 0.0, part.T)


def eliminate(groups, k, m, solve):
    rows = 8
    lane, sub = iota((rows, B), 1), iota((rows, B), 0)
    at, inside = k // rows, k % rows
    spread = lambda v: jnp.broadcast_to(v, (rows, B))
    cols = [[spread(g[:, k + i : k + i + 1]) for g in groups] for i in range(m)]
    pivot = [[spread(cols[j][at][inside + i : inside + i + 1, :]) for j in range(m)] for i in range(m)]
    inv = solve(pivot)
    lines = [spread(groups[at][inside + i : inside + i + 1, :]) for i in range(m)]
    fresh_lines = []
    for i in range(m):
        line = inv[i][0] * lines[0]
        for j in range(1, m):
            line = line + inv[i][j] * lines[j]
        for j in range(m):
            line = jnp.where(lane == k + j, inv[i][j], line)
        fresh_lines.append(line)
    out = []
    inner = (lane >= k) & (lane < k + m)
    for g in range(B // rows):
        new = jnp.where(inner, 0.0, groups[g])
        for i in range(m):
            new = new - cols[i][g] * fresh_lines[i]
        if g == at:
            for i in range(m):
                new = jnp.where(sub == inside + i, fresh_lines[i], new)
        out.append(new)
    return out


def solve2(p):
    a, b, c = p[0][0], p[0][1], p[1][1]
    scale = 1.0 / (a * c - b * b)
    off = -b * scale
    return [[c * scale, off], [off, a * scale]]


def solve4(p):
    e = solve2([p[0][:2], p[1][:2]])
    f = [row[2:] for row in p[:2]]
    m = [[e[i][0] * f[0][j] + e[i][1] * f[1][j] for j in range(2)] for i in range(2)]
    s = [[p[2 + i][2 + j] - (f[0][i] * m[0][j] + f[1][i] * m[1][j]) for j in range(2)] for i in range(2)]
    si = solve2(s)
    x = [[m[i][0] * si[0][j] + m[i][1] * si[1][j] for j in range(2)] for i in range(2)]
    top = [[e[i][j] + x[i][0] * m[j][0] + x[i][1] * m[j][1] for j in range(2)] + [-x[i][0], -x[i][1]] for i in range(2)]
    low = [[-x[0][i], -x[1][i]] + si[i] for i in range(2)]
    return top + low


def invert(mat):
    groups = [mat[g * 8 : (g + 1) * 8, :] for g in range(B // 8)]
    for k in range(0, B, 4):
        groups = eliminate(groups, k, 4, solve4)
    return jnp.concatenate(groups, axis=0)


def slot_grams(live, want, table_ref, acts_ref, grads_ref, out_ref):
    in_blocks = acts_ref.shape[1] // B
    out_blocks = grads_ref.shape[1] // B
    group_rows = 8 * H + EXTRA
    unroll = 2

    @pl.loop(0, 16 // unroll)
    def _(trip):
        for inner in range(unroll):
            group = trip * unroll + inner
            base = pl.multiple_of(group * group_rows, 16)
            diags = jnp.zeros((8, B), F32)
            for row in range(8):
                which = table_ref[(group * 2 + want) * 8 + row]
                filled = jnp.where(which >= 0, live, 0)
                first = pl.multiple_of(jnp.clip(which, 0, in_blocks - 1) * B, B)
                second = pl.multiple_of(jnp.clip(which - in_blocks, 0, out_blocks - 1) * B, B)
                x = jnp.where(which < in_blocks, acts_ref[:, pl.ds(first, B)], grads_ref[:, pl.ds(second, B)])
                x = jnp.where(iota(x.shape, 0) < filled, x, jnp.zeros_like(x))
                gram = lax.dot_general(x, x, (((0,), (0,)), ((), ())), preferred_element_type=F32)
                half, diag = pack(gram)
                out_ref[pl.ds(base + row * H, H), :] = half.astype(BF)
                diags = jnp.where(iota((8, B), 0) == row, diag, diags)
            count = jnp.full((8, B), live, jnp.int32).astype(F32)
            out_ref[pl.ds(base + 8 * H, EXTRA), :] = jnp.concatenate((diags, count), axis=0).astype(BF)


def make_plan(in_blocks, row_blocks, col_blocks, table_ref, crowd_ref, plan_ref):
    core, chip = lax.axis_index("c"), lax.axis_index("y") * 4 + lax.axis_index("x")
    wide = 2 * col_blocks
    count = wide + row_blocks
    which, lane = iota((24, B), 0), iota((24, B), 1)
    wanted = jnp.where(
        which < wide,
        in_blocks + (lane % 16) * wide + which,
        jnp.where(which < count, (lane // 16) * row_blocks + which - wide, -2),
    )
    slots = jnp.zeros_like(wanted)
    for slot in range(table_ref.shape[0]):
        slots = jnp.where(wanted == table_ref[slot], slot, slots)
    holder = slots // 16
    ranks = jnp.zeros_like(wanted)
    for at in range(count - 1):
        same = holder == jnp.broadcast_to(holder[at : at + 1, :], holder.shape)
        ranks += jnp.where(same & (which > at), 1, 0)
    crowd_ref[0] = jnp.max(jnp.where(which < count, ranks, 0))
    sends = jnp.zeros((8, B), jnp.int32)
    for at in range(max(ROOMS)):
        chosen = (holder == chip) & (ranks == 2 * at + core) & (which < count)
        row = jnp.sum(jnp.where(chosen, slots % 16, 0), axis=0, keepdims=True)
        sends = jnp.where(iota((8, B), 0) == at, jnp.broadcast_to(row, (8, B)), sends)
    plan_ref[:8, :] = sends
    plan_ref[8:32, :] = (holder * 2 + ranks % 2) * 8 + ranks // 2
    plan_ref[32:, :] = slots


def away_kernel(
    row_blocks, col_blocks, table_ref, live_ref, acts_ref, grads_ref, out_ref, crowd_ref, plan_ref, x_ref, y_ref, sems
):
    first = pltpu.make_async_copy(acts_ref, x_ref, sems.at[0])
    second = pltpu.make_async_copy(grads_ref, y_ref, sems.at[1])
    first.start()
    second.start()
    make_plan(acts_ref.shape[1] // B, row_blocks, col_blocks, table_ref, crowd_ref, plan_ref)
    first.wait()
    second.wait()
    slot_grams(live_ref[0], 1 - lax.axis_index("c"), table_ref, x_ref, y_ref, out_ref)


def own_kernel(table_ref, live_ref, acts_ref, grads_ref, out_ref):
    slot_grams(live_ref[0], lax.axis_index("c"), table_ref, acts_ref, grads_ref, out_ref)


GRAMS = jax.ShapeDtypeStruct((16 * (8 * H + EXTRA), B), BF)


def away_grams(table, live, acts, grads_out, row_blocks, col_blocks):
    return pl.pallas_call(
        functools.partial(away_kernel, row_blocks, col_blocks),
        out_shape=(
            GRAMS,
            jax.ShapeDtypeStruct((1,), jnp.int32),
            jax.ShapeDtypeStruct((56, B), jnp.int32),
            jax.ShapeDtypeStruct(acts.shape, acts.dtype),
            jax.ShapeDtypeStruct(grads_out.shape, grads_out.dtype),
        ),
        in_specs=[SMEM, SMEM, HBM, HBM],
        out_specs=(VMEM, SMEM, VMEM, VMEM, VMEM),
        scratch_shapes=[pltpu.SemaphoreType.DMA((2,))],
        compiler_params=PARAMS,
        cost_estimate=pl.CostEstimate(flops=0, bytes_accessed=36 * 2**20, transcendentals=0),
        name="grams_away",
    )(table, live, acts, grads_out)


def own_grams(table, live, acts, grads_out):
    return pl.pallas_call(
        own_kernel,
        out_shape=GRAMS,
        in_specs=[SMEM, SMEM, VMEM, VMEM],
        out_specs=VMEM,
        compiler_params=PARAMS,
        cost_estimate=pl.CostEstimate(flops=0, bytes_accessed=18 * 2**20, transcendentals=0),
        name="grams_own",
    )(table, live, acts, grads_out)


def section_kernel(parts_ref, out_ref):
    for row in range(8):
        total = parts_ref[0, row * H : (row + 1) * H, :].astype(F32)
        for g in range(1, 16):
            total += parts_ref[g, row * H : (row + 1) * H, :].astype(F32)
        out_ref[row, :H, :] = total.astype(BF)
    extra = parts_ref[0, 8 * H :, :].astype(F32)
    for g in range(1, 16):
        extra += parts_ref[g, 8 * H :, :].astype(F32)
    count = extra[8:, :]
    high = jnp.floor(count * (1.0 / 256.0))
    low = count - 256.0 * high
    sub = iota((8, B), 0)
    for row in range(8):
        first = jnp.where(sub == 0, jnp.broadcast_to(extra[row : row + 1, :], (8, B)), jnp.where(sub == 1, high, low))
        out_ref[row, H:, :] = jnp.concatenate((first, jnp.zeros_like(first)), axis=0).astype(BF)


def section_sum(parts):
    return pl.pallas_call(
        section_kernel,
        out_shape=jax.ShapeDtypeStruct((8, H + EXTRA, B), BF),
        compiler_params=pltpu.CompilerParams(vmem_limit_bytes=VMEM_LIMIT),
        name="section_sum",
    )(parts)


def take_row(rows, at):
    return jnp.sum(jnp.where(iota((EXTRA, B), 0) == at, rows, 0.0), axis=0, keepdims=True)


def inverse_kernel(parts_ref, old_ref, cov_ref, out_ref, new_ref, sem):
    half = parts_ref[0, :H, :].astype(F32)
    extra = parts_ref[0, H:, :].astype(F32)
    for s in range(1, 8):
        half += parts_ref[s, :H, :].astype(F32)
        extra += parts_ref[s, H:, :].astype(F32)
    total = extra[1:2, :] * 256.0 + extra[2:3, :]
    gram = unpack(half, extra[:1, :])
    cov = 0.8 * old_ref[0, 0] + 0.2 * gram / total
    new_ref[0, 0] = cov
    copy = pltpu.make_async_copy(new_ref, cov_ref, sem)
    copy.start()
    eye = jnp.where(iota((B, B), 0) == iota((B, B), 1), 0.1, 0.0)
    inv_half, inv_diag = pack(invert(cov + eye))
    packed = jnp.concatenate((inv_half, jnp.broadcast_to(inv_diag, (EXTRA, B))), axis=0).astype(BF)
    for section in range(8):
        out_ref[section] = packed
    copy.wait()


def inverse(parts, old_cov):
    return pl.pallas_call(
        inverse_kernel,
        out_shape=(
            jax.ShapeDtypeStruct(old_cov.shape, F32),
            jax.ShapeDtypeStruct((8, H + EXTRA, B), BF),
        ),
        in_specs=[VMEM, VMEM],
        out_specs=(HBM, VMEM),
        scratch_shapes=[pltpu.VMEM(old_cov.shape, F32), pltpu.SemaphoreType.DMA],
        compiler_params=PARAMS,
        name="inverse",
    )(parts, old_cov)


def route_kernel(room, plan_ref, mine_ref, other_ref, out_ref):
    core, lane = lax.axis_index("c"), lax.axis_index("z") * 16
    for chip in range(16):
        diags = jnp.zeros((EXTRA, B), F32)
        for at in range(room):
            if room in ROOMS:
                index = plan_ref[at, lane + chip]
                block = jnp.where(index // 8 == core, mine_ref[index % 8], other_ref[index % 8])
            else:
                block = mine_ref[at]
            out_ref[chip, at * H : (at + 1) * H, :] = block[:H, :]
            diags = jnp.where(iota((EXTRA, B), 0) == at, block[H:, :].astype(F32), diags)
        out_ref[chip, room * H :, :] = diags.astype(BF)


def route(room, plans, mine, other):
    return pl.pallas_call(
        functools.partial(route_kernel, room),
        out_shape=jax.ShapeDtypeStruct((16, room * H + EXTRA, B), BF),
        in_specs=[SMEM, VMEM, VMEM],
        out_specs=VMEM,
        compiler_params=PARAMS,
        name="route",
    )(plans, mine, other)


def final_kernel(room, plan_ref, mine_ref, other_ref, weight_ref, out_ref, left_ref, right_ref, sems):
    core = lax.axis_index("c")
    lane = lax.axis_index("z") * 16 + lax.axis_index("y") * 4 + lax.axis_index("x")
    row_blocks = weight_ref.shape[0] // B
    col_blocks = weight_ref.shape[1] // B

    def block(index):
        found = plan_ref[(8 if room in ROOMS else 32) + index, lane]
        holder, at = found // 8, found % 8
        same = holder % 2 == core
        chip = holder // 2
        rows = pl.ds(pl.multiple_of(at * H, H), H)
        half = jnp.where(same, mine_ref[chip, rows, :], other_ref[chip, rows, :]).astype(F32)
        diags = jnp.where(same, mine_ref[chip, room * H :, :], other_ref[chip, room * H :, :]).astype(F32)
        return unpack(half, take_row(diags, at)).astype(BF)

    col_invs = [block(core * col_blocks + j) for j in range(col_blocks)]
    copies = []
    strips = 2
    for strip in range(strips):
        span = row_blocks // strips
        for i in range(strip * span, (strip + 1) * span):
            rows = slice(i * B, (i + 1) * B)
            left = jnp.dot(block(2 * col_blocks + i), weight_ref[rows, :], preferred_element_type=F32)
            left_ref[rows, :] = left.astype(BF)
        rows = slice(strip * span * B, (strip + 1) * span * B)
        for j in range(col_blocks):
            cols = slice(j * B, (j + 1) * B)
            right = jnp.dot(left_ref[rows, cols], col_invs[j], preferred_element_type=F32)
            right_ref[rows, cols] = right.astype(BF)
        copies.append(pltpu.make_async_copy(right_ref.at[rows, :], out_ref.at[rows, :], sems.at[strip]))
        copies[-1].start()
    for copy in copies:
        copy.wait()


def final(room, plans, mine, other, weight_grad):
    return pl.pallas_call(
        functools.partial(final_kernel, room),
        out_shape=jax.ShapeDtypeStruct(weight_grad.shape, BF),
        in_specs=[SMEM, VMEM, VMEM, VMEM],
        out_specs=HBM,
        scratch_shapes=[
            pltpu.VMEM(weight_grad.shape, BF),
            pltpu.VMEM(weight_grad.shape, BF),
            pltpu.SemaphoreType.DMA((2,)),
        ],
        compiler_params=PARAMS,
        name="final",
    )(plans, mine, other, weight_grad)


def on_device(acts, grads_out, weight_grad, slot_table, row_counts, old_cov):
    row_blocks = weight_grad.shape[0] // B
    col_blocks = weight_grad.shape[1] // B
    plane = ("y", "x")
    exchange = functools.partial(lax.all_to_all, split_axis=0, concat_axis=0, tiled=True)
    swap = functools.partial(lax.ppermute, axis_name="c", perm=[(0, 1), (1, 0)])

    away, crowd, plans, acts_held, grads_held = away_grams(
        slot_table, row_counts, acts, grads_out, row_blocks, col_blocks
    )
    got = swap(away)
    own = own_grams(slot_table, row_counts, acts_held, grads_held)
    sums = (own.astype(F32) + got.astype(F32)).astype(BF)
    branch = sum((crowd[0] >= 2 * room).astype(jnp.int32) for room in ROOMS)
    sums, branch = lax.optimization_barrier((sums, branch))
    parts = exchange(sums.reshape(16, -1, B), plane)
    parts = exchange(section_sum(parts), "z")
    new_cov, inv = inverse(parts, old_cov)
    mine = exchange(inv, "z")

    def compact(room, plans, mine, weight_grad):
        got = exchange(route(room, plans, mine, swap(mine)), plane)
        return final(room, plans, got, swap(got), weight_grad)

    def full(plans, mine, weight_grad):
        got = exchange(route(8, plans, mine, mine), plane)
        return final(8, plans, got, swap(got), weight_grad)

    branches = [functools.partial(compact, room) for room in ROOMS] + [full]
    return lax.switch(branch, branches, plans, mine, weight_grad), new_cov


def solution(mesh):
    wide = Mesh(mesh.devices.reshape(8, 4, 4, 2), ("z", "y", "x", "c"))
    dp = ("y", "x", "c")
    in_specs = (
        P(("z",) + dp, None),
        P(("z",) + dp, None),
        P("z", dp),
        P(),
        P(("z",) + dp),
        P(dp, "z", None, None),
    )
    out_specs = (P("z", dp), P(dp, "z", None, None))
    return jax.shard_map(
        on_device, mesh=wide, in_specs=in_specs, out_specs=out_specs, check_vma=False
    )
```

```python
import functools

import jax
import jax.numpy as jnp
import numpy as np
from jax import lax
from jax.experimental import pallas as pl
from jax.experimental.pallas import tpu as pltpu
from jax.sharding import Mesh, PartitionSpec as P

B = 128
H = B // 2
BF = jnp.bfloat16
F32 = jnp.float32
EXTRA = 16
ROOMS = (3, 4)
PARTS = 3
STRIPS = 2
VMEM_LIMIT = 24 * 1024 * 1024


SMEM = pl.BlockSpec(memory_space=pltpu.SMEM)
VMEM = pl.BlockSpec(memory_space=pltpu.VMEM)
HBM = pl.BlockSpec(memory_space=pltpu.HBM)
PARAMS = pltpu.CompilerParams(vmem_limit_bytes=VMEM_LIMIT)


def iota(shape, dim):
    return lax.broadcasted_iota(jnp.int32, shape, dim)


def pack(sym):
    top = sym[:H, :]
    low = pltpu.roll(sym[H:, :], H, 1)
    row, lane = iota((H, B), 0), iota((H, B), 1)
    half = jnp.where(lane < row, low, top)
    diag = jnp.sum(jnp.where(lane == row, low, 0.0), axis=0, keepdims=True)
    return half, diag


def unpack(half, diag):
    row, lane = iota((H, B), 0), iota((H, B), 1)
    upper = jnp.where(lane >= row, half, 0.0)
    lower = jnp.where(lane < row, half, 0.0)
    lower = jnp.where(lane == row, diag, lower)
    lower = pltpu.roll(lower, H, 1)
    part = jnp.concatenate((upper, lower), axis=0)
    brow, blane = iota((B, B), 0), iota((B, B), 1)
    return part + jnp.where(brow == blane, 0.0, part.T)


def eliminate(strips, first, k, m, solve):
    rows = 8
    lane, sub = iota((rows, B), 1), iota((rows, B), 0)
    at, inside = (k - first) // rows, k % rows
    spread = lambda v: jnp.broadcast_to(v, (rows, B))
    cols = [[spread(s[:, k + i : k + i + 1]) for s in strips] for i in range(m)]
    pivot = [[spread(cols[j][at][inside + i : inside + i + 1, :]) for j in range(m)] for i in range(m)]
    inv = solve(pivot)
    lines = [spread(strips[at][inside + i : inside + i + 1, :]) for i in range(m)]
    fresh = []
    for i in range(m):
        line = inv[i][0] * lines[0]
        for j in range(1, m):
            line = line + inv[i][j] * lines[j]
        for j in range(m):
            line = jnp.where(lane == k + j, inv[i][j], line)
        fresh.append(line)
    out = []
    pivots = (lane >= k) & (lane < k + m)
    for g, strip in enumerate(strips):
        new = jnp.where(pivots, 0.0, strip)
        for i in range(m):
            new = new - cols[i][g] * fresh[i]
        if g == at:
            for i in range(m):
                new = jnp.where(sub == inside + i, fresh[i], new)
        out.append(new)
    return out


def solve2(p):
    a, b, c = p[0][0], p[0][1], p[1][1]
    scale = 1.0 / (a * c - b * b)
    off = -b * scale
    return [[c * scale, off], [off, a * scale]]


def solve4(p):
    e = solve2([p[0][:2], p[1][:2]])
    f = [row[2:] for row in p[:2]]
    m = [[e[i][0] * f[0][j] + e[i][1] * f[1][j] for j in range(2)] for i in range(2)]
    s = [[p[2 + i][2 + j] - (f[0][i] * m[0][j] + f[1][i] * m[1][j]) for j in range(2)] for i in range(2)]
    si = solve2(s)
    x = [[m[i][0] * si[0][j] + m[i][1] * si[1][j] for j in range(2)] for i in range(2)]
    top = [[e[i][j] + x[i][0] * m[j][0] + x[i][1] * m[j][1] for j in range(2)] + [-x[i][0], -x[i][1]] for i in range(2)]
    low = [[-x[0][i], -x[1][i]] + si[i] for i in range(2)]
    return top + low


def product(a, b):
    return [[sum(a[i][t] * b[t][j] for t in range(1, len(b))) + a[i][0] * b[0][j] for j in range(len(b[0]))] for i in range(len(a))]


def turned(a):
    return [list(row) for row in zip(*a)]


def solve8(p):
    e = solve4([row[:4] for row in p[:4]])
    f = [row[4:] for row in p[:4]]
    m = product(e, f)
    fm = product(turned(f), m)
    si = solve4([[p[4 + i][4 + j] - fm[i][j] for j in range(4)] for i in range(4)])
    x = product(m, si)
    xm = product(x, turned(m))
    top = [[e[i][j] + xm[i][j] for j in range(4)] + [-x[i][j] for j in range(4)] for i in range(4)]
    low = [[-x[j][i] for j in range(4)] + si[i] for i in range(4)]
    return top + low


def invert(mat):
    size = 32
    dot = functools.partial(jnp.dot, precision=lax.Precision.HIGHEST, preferred_element_type=F32)
    row, lane = iota((B, B), 0), iota((B, B), 1)
    for first in range(0, B, size):
        across = (lane >= first) & (lane < first + size)
        down = (row >= first) & (row < first + size)
        own = jnp.where(across, mat, 0.0)
        strips = [own[first + g : first + g + 8, :] for g in range(0, size, 8)]
        for k in range(first, first + size, 8):
            strips = eliminate(strips, first, k, 8, solve8)
        block = jnp.concatenate(strips, axis=0)
        lines = jnp.where(across[:size], block, dot(block, mat))
        edges = [jnp.zeros((rows, B), F32) for rows in (first, B - first - size)]
        lines = jnp.concatenate([part for part in (edges[0], lines, edges[1]) if part.shape[0]], axis=0)
        mat = jnp.where(down, lines, jnp.where(across, 0.0, mat) - dot(own, lines))
    return mat


def slot_grams(live, want, table_ref, acts_ref, grads_ref, out_ref):
    in_blocks = acts_ref.shape[1] // B
    out_blocks = grads_ref.shape[1] // B
    group_rows = 8 * H + EXTRA
    unroll = 4

    @pl.loop(0, 16 // unroll)
    def _(trip):
        for inner in range(unroll):
            group = trip * unroll + inner
            base = pl.multiple_of(group * group_rows, 16)
            diags = jnp.zeros((8, B), F32)
            for row in range(8):
                which = table_ref[(group * 2 + want) * 8 + row]
                filled = jnp.where(which >= 0, live, 0)
                first = pl.multiple_of(jnp.clip(which, 0, in_blocks - 1) * B, B)
                second = pl.multiple_of(jnp.clip(which - in_blocks, 0, out_blocks - 1) * B, B)
                x = jnp.where(which < in_blocks, acts_ref[:, pl.ds(first, B)], grads_ref[:, pl.ds(second, B)])
                x = jnp.where(iota(x.shape, 0) < filled, x, jnp.zeros_like(x))
                gram = lax.dot_general(x, x, (((0,), (0,)), ((), ())), preferred_element_type=F32)
                half, diag = pack(gram)
                out_ref[pl.ds(base + row * H, H), :] = half.astype(BF)
                diags = jnp.where(iota((8, B), 0) == row, diag, diags)
            count = jnp.full((8, B), live, jnp.int32).astype(F32)
            out_ref[pl.ds(base + 8 * H, EXTRA), :] = jnp.concatenate((diags, count), axis=0).astype(BF)


def make_plan(in_blocks, row_blocks, col_blocks, table_ref, branch_ref, send_ref, find_ref, turned_ref):
    core, chip = lax.axis_index("c"), lax.axis_index("y") * 4 + lax.axis_index("x")
    wide = 2 * col_blocks
    count = wide + row_blocks
    which, lane = iota((24, B), 0), iota((24, B), 1)
    wanted = jnp.where(
        which < wide,
        in_blocks + (lane % 16) * wide + which,
        jnp.where(which < count, (lane // 16) * row_blocks + which - wide, -2),
    )
    slots = jnp.zeros_like(wanted)
    for slot in range(table_ref.shape[0]):
        slots = jnp.where(wanted == table_ref[slot], slot, slots)
    holder = slots // 16
    ranks = jnp.zeros_like(wanted)
    for at in range(count - 1):
        same = holder == jnp.broadcast_to(holder[at : at + 1, :], holder.shape)
        ranks += jnp.where(same & (which > at), 1, 0)
    most = jnp.max(jnp.where(which < count, ranks, 0))
    branch_ref[0] = sum((most >= 2 * room).astype(jnp.int32) for room in ROOMS)
    sends = jnp.zeros((8, B), jnp.int32)
    for at in range(max(ROOMS)):
        chosen = (holder == chip) & (ranks == 2 * at + core) & (which < count)
        row = jnp.sum(jnp.where(chosen, slots % 16, 0), axis=0, keepdims=True)
        sends = jnp.where(iota((8, B), 0) == at, jnp.broadcast_to(row, (8, B)), sends)
    finds = (holder * 2 + ranks % 2) * 8 + ranks // 2
    rest = jnp.zeros((B - 56, B), jnp.int32)
    turned_ref[...] = jnp.concatenate((sends, finds, slots, rest), axis=0).T
    section = lax.axis_index("z") * 16
    send_ref[...] = turned_ref[pl.ds(pl.multiple_of(section, 16), 16), :]
    find_ref[...] = jnp.broadcast_to(turned_ref[pl.ds(section + chip, 1), :], find_ref.shape)


def away_kernel(
    row_blocks, col_blocks, table_ref, live_ref, acts_ref, grads_ref,
    out_ref, branch_ref, send_ref, find_ref, x_ref, y_ref,
    held_ref, turned_ref, sems,
):
    lookup = pltpu.make_async_copy(table_ref, held_ref, sems.at[PARTS + 1])
    lookup.start()
    copies = [pltpu.make_async_copy(acts_ref, x_ref, sems.at[0])]
    width = grads_ref.shape[1] // PARTS
    for part in range(PARTS):
        cols = slice(part * width, (part + 1) * width)
        copies.append(pltpu.make_async_copy(grads_ref.at[:, cols], y_ref.at[:, cols], sems.at[part + 1]))
    for copy in copies:
        copy.start()
    lookup.wait()
    make_plan(acts_ref.shape[1] // B, row_blocks, col_blocks, held_ref, branch_ref, send_ref, find_ref, turned_ref)
    for copy in copies:
        copy.wait()
    slot_grams(live_ref[0], 1 - lax.axis_index("c"), held_ref, x_ref, y_ref, out_ref)


def own_kernel(table_ref, live_ref, acts_ref, grads_ref, out_ref):
    slot_grams(live_ref[0], lax.axis_index("c"), table_ref, acts_ref, grads_ref, out_ref)


GRAMS = jax.ShapeDtypeStruct((16 * (8 * H + EXTRA), B), BF)


def away_grams(table, live, acts, grads_out, row_blocks, col_blocks):
    return pl.pallas_call(
        functools.partial(away_kernel, row_blocks, col_blocks),
        out_shape=(
            GRAMS,
            jax.ShapeDtypeStruct((1,), jnp.int32),
            jax.ShapeDtypeStruct((16, B), jnp.int32),
            jax.ShapeDtypeStruct((8, B), jnp.int32),
            jax.ShapeDtypeStruct(acts.shape, acts.dtype),
            jax.ShapeDtypeStruct(grads_out.shape, grads_out.dtype),
        ),
        in_specs=[HBM, SMEM, HBM, HBM],
        out_specs=(VMEM, SMEM, VMEM, VMEM, VMEM, VMEM),
        scratch_shapes=[
            pltpu.SMEM(table.shape, jnp.int32),
            pltpu.VMEM((B, B), jnp.int32),
            pltpu.SemaphoreType.DMA((PARTS + 2,)),
        ],
        compiler_params=PARAMS,
        cost_estimate=pl.CostEstimate(flops=0, bytes_accessed=36 * 2**20, transcendentals=0),
        name="grams_away",
    )(
        pltpu.with_memory_space_constraint(table, pltpu.HBM),
        live,
        pltpu.with_memory_space_constraint(acts, pltpu.HBM),
        pltpu.with_memory_space_constraint(grads_out, pltpu.HBM),
    )


def own_grams(table, live, acts, grads_out):
    return pl.pallas_call(
        own_kernel,
        out_shape=GRAMS,
        in_specs=[SMEM, SMEM, VMEM, VMEM],
        out_specs=VMEM,
        compiler_params=PARAMS,
        cost_estimate=pl.CostEstimate(flops=0, bytes_accessed=18 * 2**20, transcendentals=0),
        name="grams_own",
    )(table, live, acts, grads_out)


def section_kernel(parts_ref, out_ref):
    for row in range(8):
        total = parts_ref[0, row * H : (row + 1) * H, :].astype(F32)
        for g in range(1, 16):
            total += parts_ref[g, row * H : (row + 1) * H, :].astype(F32)
        out_ref[row, :H, :] = total.astype(BF)
    extra = parts_ref[0, 8 * H :, :].astype(F32)
    for g in range(1, 16):
        extra += parts_ref[g, 8 * H :, :].astype(F32)
    count = extra[8:, :]
    high = jnp.floor(count * (1.0 / 256.0))
    low = count - 256.0 * high
    sub = iota((8, B), 0)
    for row in range(8):
        first = jnp.where(sub == 0, jnp.broadcast_to(extra[row : row + 1, :], (8, B)), jnp.where(sub == 1, high, low))
        out_ref[row, H:, :] = jnp.concatenate((first, jnp.zeros_like(first)), axis=0).astype(BF)


def section_sum(parts):
    return pl.pallas_call(
        section_kernel,
        out_shape=jax.ShapeDtypeStruct((8, H + EXTRA, B), BF),
        compiler_params=pltpu.CompilerParams(vmem_limit_bytes=VMEM_LIMIT),
        name="section_sum",
    )(parts)


def take_row(rows, at):
    return jnp.sum(jnp.where(iota((EXTRA, B), 0) == at, rows, 0.0), axis=0, keepdims=True)


def inverse_kernel(parts_ref, old_ref, cov_ref, out_ref):
    half = parts_ref[0, :H, :].astype(F32)
    extra = parts_ref[0, H:, :].astype(F32)
    for s in range(1, 8):
        half += parts_ref[s, :H, :].astype(F32)
        extra += parts_ref[s, H:, :].astype(F32)
    total = extra[1:2, :] * 256.0 + extra[2:3, :]
    gram = unpack(half, extra[:1, :])
    cov = 0.8 * old_ref[0, 0] + 0.2 * gram / total
    cov_ref[0, 0] = cov
    eye = jnp.where(iota((B, B), 0) == iota((B, B), 1), 0.1, 0.0)
    inv_half, inv_diag = pack(invert(cov + eye))
    packed = jnp.concatenate((inv_half, jnp.broadcast_to(inv_diag, (EXTRA, B))), axis=0).astype(BF)
    for section in range(8):
        out_ref[section] = packed


def inverse(parts, old_cov):
    return pl.pallas_call(
        inverse_kernel,
        out_shape=(
            jax.ShapeDtypeStruct(old_cov.shape, F32),
            jax.ShapeDtypeStruct((8, H + EXTRA, B), BF),
        ),
        in_specs=[VMEM, VMEM],
        out_specs=(VMEM, VMEM),
        compiler_params=PARAMS,
        name="inverse",
    )(parts, old_cov)


def route_kernel(room, send_ref, mine_ref, other_ref, out_ref):
    core = lax.axis_index("c")
    for chip in range(16):
        diags = jnp.zeros((EXTRA, B), F32)
        for at in range(room):
            if room in ROOMS:
                index = send_ref[chip, at]
                block = jnp.where(index // 8 == core, mine_ref[index % 8], other_ref[index % 8])
            else:
                block = mine_ref[at]
            out_ref[chip, at * H : (at + 1) * H, :] = block[:H, :]
            diags = jnp.where(iota((EXTRA, B), 0) == at, block[H:, :].astype(F32), diags)
        out_ref[chip, room * H :, :] = diags.astype(BF)


def route(room, sends, mine, other):
    return pl.pallas_call(
        functools.partial(route_kernel, room),
        out_shape=jax.ShapeDtypeStruct((16, room * H + EXTRA, B), BF),
        in_specs=[SMEM, VMEM, VMEM],
        out_specs=VMEM,
        compiler_params=PARAMS,
        name="route",
    )(sends, mine, other)


def pick_kernel(room, col_blocks, find_ref, got_ref, keep_ref, give_ref):
    core = lax.axis_index("c")
    for ref, column in ((keep_ref, core), (give_ref, 1 - core)):
        for want in range(ref.shape[0]):
            index = column * col_blocks + want if want < col_blocks else col_blocks + want
            found = find_ref[0, (8 if room in ROOMS else 32) + index]
            chip, at = found // 16, found % 8
            rows = pl.ds(pl.multiple_of(at * H, H), H)
            ref[want, :H, :] = got_ref[chip, rows, :]
            diag = take_row(got_ref[chip, room * H :, :].astype(F32), at)
            ref[want, H:, :] = jnp.broadcast_to(diag, (EXTRA, B)).astype(BF)


def pick(room, finds, got, row_blocks, col_blocks):
    out = jax.ShapeDtypeStruct((col_blocks + row_blocks, H + EXTRA, B), BF)
    return pl.pallas_call(
        functools.partial(pick_kernel, room, col_blocks),
        out_shape=(out, out),
        in_specs=[SMEM, VMEM],
        out_specs=(VMEM, VMEM),
        compiler_params=PARAMS,
        name="pick",
    )(finds, got)


def final_kernel(find_ref, branch_ref, mine_ref, other_ref, weight_ref, out_ref, left_ref, right_ref, sems):
    core = lax.axis_index("c")
    row_blocks = weight_ref.shape[0] // B
    col_blocks = weight_ref.shape[1] // B
    base = jnp.where(branch_ref[0] < len(ROOMS), 8, 32)

    def block(want, index):
        same = (find_ref[0, base + index] // 8) % 2 == core
        packed = jnp.where(same, mine_ref[want], other_ref[want]).astype(F32)
        return unpack(packed[:H, :], packed[H : H + 1, :]).astype(BF)

    col_invs = [block(j, core * col_blocks + j) for j in range(col_blocks)]
    copies = []
    span = row_blocks // STRIPS
    for strip in range(STRIPS):
        for i in range(strip * span, (strip + 1) * span):
            rows = slice(i * B, (i + 1) * B)
            inv = block(col_blocks + i, 2 * col_blocks + i)
            left = jnp.dot(inv, weight_ref[rows, :], preferred_element_type=F32)
            left_ref[rows, :] = left.astype(BF)
        rows = slice(strip * span * B, (strip + 1) * span * B)
        for j in range(col_blocks):
            cols = slice(j * B, (j + 1) * B)
            right = jnp.dot(left_ref[rows, cols], col_invs[j], preferred_element_type=F32)
            right_ref[rows, cols] = right.astype(BF)
        copies.append(pltpu.make_async_copy(right_ref.at[rows, :], out_ref.at[rows, :], sems.at[strip]))
        copies[-1].start()
    for copy in copies:
        copy.wait()


def final(finds, branch, mine, other, weight_grad):
    return pl.pallas_call(
        final_kernel,
        out_shape=jax.ShapeDtypeStruct(weight_grad.shape, BF),
        in_specs=[SMEM, SMEM, VMEM, VMEM, VMEM],
        out_specs=HBM,
        scratch_shapes=[
            pltpu.VMEM(weight_grad.shape, BF),
            pltpu.VMEM(weight_grad.shape, BF),
            pltpu.SemaphoreType.DMA((STRIPS,)),
        ],
        compiler_params=PARAMS,
        name="final",
    )(finds, branch, mine, other, weight_grad)


def on_device(acts, grads_out, weight_grad, slot_table, row_counts, old_cov):
    row_blocks = weight_grad.shape[0] // B
    col_blocks = weight_grad.shape[1] // B
    plane = ("y", "x")
    exchange = functools.partial(lax.all_to_all, split_axis=0, concat_axis=0, tiled=True)
    swap = functools.partial(lax.ppermute, axis_name="c", perm=[(0, 1), (1, 0)])

    away, branch, sends, finds, acts_held, grads_held = away_grams(
        slot_table, row_counts, acts, grads_out, row_blocks, col_blocks
    )
    got = swap(away)
    own = own_grams(slot_table, row_counts, acts_held, grads_held)
    sums = (own.astype(F32) + got.astype(F32)).astype(BF)
    parts = exchange(sums.reshape(16, -1, B), plane)
    parts = exchange(section_sum(parts), "z")
    new_cov, inv = inverse(parts, old_cov)
    mine = exchange(inv, "z")

    def compact(room, sends, finds, mine):
        got = exchange(route(room, sends, mine, swap(mine)), plane)
        return pick(room, finds, got, row_blocks, col_blocks)

    def full(sends, finds, mine):
        got = exchange(route(8, sends, mine, mine), plane)
        return pick(8, finds, got, row_blocks, col_blocks)

    branches = [functools.partial(compact, room) for room in ROOMS] + [full]
    keep, give = lax.switch(branch[0], branches, sends, finds, mine)
    return final(finds, branch, keep, swap(give), weight_grad), new_cov


def solution(mesh):
    wide = Mesh(mesh.devices.reshape(8, 4, 4, 2), ("z", "y", "x", "c"))
    dp = ("y", "x", "c")
    in_specs = (
        P(("z",) + dp, None),
        P(("z",) + dp, None),
        P("z", dp),
        P(),
        P(("z",) + dp),
        P(dp, "z", None, None),
    )
    out_specs = (P("z", dp), P(dp, "z", None, None))
    return jax.shard_map(
        on_device, mesh=wide, in_specs=in_specs, out_specs=out_specs, check_vma=False
    )
```

```python
import functools

import jax
import jax.numpy as jnp
import numpy as np
from jax import lax
from jax.experimental import pallas as pl
from jax.experimental.pallas import tpu as pltpu
from jax.sharding import Mesh, PartitionSpec as P

B = 128
H = B // 2
BF = jnp.bfloat16
F32 = jnp.float32
EXTRA = 16
ROOMS = (3, 4)
PARTS = 6
STRIPS = 2
VMEM_LIMIT = 24 * 1024 * 1024


SMEM = pl.BlockSpec(memory_space=pltpu.SMEM)
VMEM = pl.BlockSpec(memory_space=pltpu.VMEM)
HBM = pl.BlockSpec(memory_space=pltpu.HBM)
PARAMS = pltpu.CompilerParams(vmem_limit_bytes=VMEM_LIMIT)


def iota(shape, dim):
    return lax.broadcasted_iota(jnp.int32, shape, dim)


def pack(sym):
    top = sym[:H, :]
    low = pltpu.roll(sym[H:, :], H, 1)
    row, lane = iota((H, B), 0), iota((H, B), 1)
    half = jnp.where(lane < row, low, top)
    diag = jnp.sum(jnp.where(lane == row, low, 0.0), axis=0, keepdims=True)
    return half, diag


def unpack(half, diag):
    row, lane = iota((H, B), 0), iota((H, B), 1)
    upper = jnp.where(lane >= row, half, 0.0)
    lower = jnp.where(lane < row, half, 0.0)
    lower = jnp.where(lane == row, diag, lower)
    lower = pltpu.roll(lower, H, 1)
    part = jnp.concatenate((upper, lower), axis=0)
    brow, blane = iota((B, B), 0), iota((B, B), 1)
    return part + jnp.where(brow == blane, 0.0, part.T)


def eliminate(strips, first, k, m, solve):
    rows = 8
    lane, sub = iota((rows, B), 1), iota((rows, B), 0)
    at, inside = (k - first) // rows, k % rows
    spread = lambda v: jnp.broadcast_to(v, (rows, B))
    cols = [[spread(s[:, k + i : k + i + 1]) for s in strips] for i in range(m)]
    pivot = [[spread(cols[j][at][inside + i : inside + i + 1, :]) for j in range(m)] for i in range(m)]
    inv = solve(pivot)
    lines = [spread(strips[at][inside + i : inside + i + 1, :]) for i in range(m)]
    fresh = []
    for i in range(m):
        line = inv[i][0] * lines[0]
        for j in range(1, m):
            line = line + inv[i][j] * lines[j]
        for j in range(m):
            line = jnp.where(lane == k + j, inv[i][j], line)
        fresh.append(line)
    out = []
    pivots = (lane >= k) & (lane < k + m)
    for g, strip in enumerate(strips):
        new = jnp.where(pivots, 0.0, strip)
        for i in range(m):
            new = new - cols[i][g] * fresh[i]
        if g == at:
            for i in range(m):
                new = jnp.where(sub == inside + i, fresh[i], new)
        out.append(new)
    return out


def solve2(p):
    a, b, c = p[0][0], p[0][1], p[1][1]
    scale = 1.0 / (a * c - b * b)
    off = -b * scale
    return [[c * scale, off], [off, a * scale]]


def solve4(p):
    e = solve2([p[0][:2], p[1][:2]])
    f = [row[2:] for row in p[:2]]
    m = [[e[i][0] * f[0][j] + e[i][1] * f[1][j] for j in range(2)] for i in range(2)]
    s = [[p[2 + i][2 + j] - (f[0][i] * m[0][j] + f[1][i] * m[1][j]) for j in range(2)] for i in range(2)]
    si = solve2(s)
    x = [[m[i][0] * si[0][j] + m[i][1] * si[1][j] for j in range(2)] for i in range(2)]
    top = [[e[i][j] + x[i][0] * m[j][0] + x[i][1] * m[j][1] for j in range(2)] + [-x[i][0], -x[i][1]] for i in range(2)]
    low = [[-x[0][i], -x[1][i]] + si[i] for i in range(2)]
    return top + low


def product(a, b):
    return [[sum(a[i][t] * b[t][j] for t in range(1, len(b))) + a[i][0] * b[0][j] for j in range(len(b[0]))] for i in range(len(a))]


def turned(a):
    return [list(row) for row in zip(*a)]


def solve8(p):
    e = solve4([row[:4] for row in p[:4]])
    f = [row[4:] for row in p[:4]]
    m = product(e, f)
    fm = product(turned(f), m)
    si = solve4([[p[4 + i][4 + j] - fm[i][j] for j in range(4)] for i in range(4)])
    x = product(m, si)
    xm = product(x, turned(m))
    top = [[e[i][j] + xm[i][j] for j in range(4)] + [-x[i][j] for j in range(4)] for i in range(4)]
    low = [[-x[j][i] for j in range(4)] + si[i] for i in range(4)]
    return top + low


def invert(mat):
    size = 32
    dot = functools.partial(jnp.dot, precision=lax.Precision.HIGHEST, preferred_element_type=F32)
    row, lane = iota((B, B), 0), iota((B, B), 1)
    for first in range(0, B, size):
        across = (lane >= first) & (lane < first + size)
        down = (row >= first) & (row < first + size)
        own = jnp.where(across, mat, 0.0)
        strips = [own[first + g : first + g + 8, :] for g in range(0, size, 8)]
        for k in range(first, first + size, 8):
            strips = eliminate(strips, first, k, 8, solve8)
        block = jnp.concatenate(strips, axis=0)
        lines = jnp.where(across[:size], block, dot(block, mat))
        edges = [jnp.zeros((rows, B), F32) for rows in (first, B - first - size)]
        lines = jnp.concatenate([part for part in (edges[0], lines, edges[1]) if part.shape[0]], axis=0)
        mat = jnp.where(down, lines, jnp.where(across, 0.0, mat) - dot(own, lines))
    return mat


def slot_grams(live, want, table_ref, x_ref, out_ref):
    blocks = x_ref.shape[1] // B
    group_rows = 8 * H + EXTRA
    unroll = 8

    @pl.loop(0, 16 // unroll)
    def _(trip):
        for inner in range(unroll):
            group = trip * unroll + inner
            base = pl.multiple_of(group * group_rows, 16)
            diags = jnp.zeros((8, B), F32)
            for row in range(8):
                which = table_ref[(group * 2 + want) * 8 + row]
                filled = jnp.where(which >= 0, live, 0)
                first = pl.multiple_of(jnp.clip(which, 0, blocks - 1) * B, B)
                x = x_ref[:, pl.ds(first, B)]
                x = jnp.where(iota(x.shape, 0) < filled, x, jnp.zeros_like(x))
                gram = lax.dot_general(x, x, (((0,), (0,)), ((), ())), preferred_element_type=F32)
                half, diag = pack(gram)
                out_ref[pl.ds(base + row * H, H), :] = half.astype(BF)
                diags = jnp.where(iota((8, B), 0) == row, diag, diags)
            count = jnp.full((8, B), live, jnp.int32).astype(F32)
            out_ref[pl.ds(base + 8 * H, EXTRA), :] = jnp.concatenate((diags, count), axis=0).astype(BF)


def make_plan(in_blocks, row_blocks, col_blocks, table_ref, branch_ref, send_ref, find_ref, turned_ref):
    core, chip = lax.axis_index("c"), lax.axis_index("y") * 4 + lax.axis_index("x")
    wide = 2 * col_blocks
    count = wide + row_blocks
    which, lane = iota((24, B), 0), iota((24, B), 1)
    wanted = jnp.where(
        which < wide,
        in_blocks + (lane % 16) * wide + which,
        jnp.where(which < count, (lane // 16) * row_blocks + which - wide, -2),
    )
    slots = jnp.zeros_like(wanted)
    for slot in range(table_ref.shape[0]):
        slots = jnp.where(wanted == table_ref[slot], slot, slots)
    holder = slots // 16
    ranks = jnp.zeros_like(wanted)
    for at in range(count - 1):
        same = holder == jnp.broadcast_to(holder[at : at + 1, :], holder.shape)
        ranks += jnp.where(same & (which > at), 1, 0)
    most = jnp.max(jnp.where(which < count, ranks, 0))
    sends = jnp.zeros((8, B), jnp.int32)
    for at in range(max(ROOMS)):
        chosen = (holder == chip) & (ranks == 2 * at + core) & (which < count)
        row = jnp.sum(jnp.where(chosen, slots % 16, 0), axis=0, keepdims=True)
        sends = jnp.where(iota((8, B), 0) == at, jnp.broadcast_to(row, (8, B)), sends)
    finds = (holder * 2 + ranks % 2) * 8 + ranks // 2
    branch = sum((most >= 2 * room).astype(jnp.int32) for room in ROOMS)
    branch_ref[0] = branch
    cores = jnp.where(branch < len(ROOMS), ranks, slots // 8) % 2
    rest = jnp.zeros((B - 80, B), jnp.int32)
    turned_ref[...] = jnp.concatenate((sends, finds, slots, cores, rest), axis=0).T
    section = lax.axis_index("z") * 16
    send_ref[...] = turned_ref[pl.ds(pl.multiple_of(section, 16), 16), :]
    find_ref[...] = jnp.broadcast_to(turned_ref[pl.ds(section + chip, 1), :], find_ref.shape)


def away_kernel(
    row_blocks, col_blocks, table_ref, live_ref, acts_ref, grads_ref,
    out_ref, branch_ref, send_ref, find_ref, x_ref,
    held_ref, turned_ref, sems,
):
    lookup = pltpu.make_async_copy(table_ref, held_ref, sems.at[PARTS + 1])
    lookup.start()
    inner = acts_ref.shape[1]
    copies = [pltpu.make_async_copy(acts_ref, x_ref.at[:, :inner], sems.at[0])]
    width = grads_ref.shape[1] // PARTS
    for part in range(PARTS):
        source = grads_ref.at[:, part * width : (part + 1) * width]
        target = x_ref.at[:, inner + part * width : inner + (part + 1) * width]
        copies.append(pltpu.make_async_copy(source, target, sems.at[part + 1]))
    for copy in copies:
        copy.start()
    lookup.wait()
    make_plan(acts_ref.shape[1] // B, row_blocks, col_blocks, held_ref, branch_ref, send_ref, find_ref, turned_ref)
    for copy in copies:
        copy.wait()
    slot_grams(live_ref[0], 1 - lax.axis_index("c"), held_ref, x_ref, out_ref)


def own_kernel(table_ref, live_ref, x_ref, out_ref):
    slot_grams(live_ref[0], lax.axis_index("c"), table_ref, x_ref, out_ref)


GRAMS = jax.ShapeDtypeStruct((16 * (8 * H + EXTRA), B), BF)


def away_grams(table, live, acts, grads_out, row_blocks, col_blocks):
    return pl.pallas_call(
        functools.partial(away_kernel, row_blocks, col_blocks),
        out_shape=(
            GRAMS,
            jax.ShapeDtypeStruct((1,), jnp.int32),
            jax.ShapeDtypeStruct((16, B), jnp.int32),
            jax.ShapeDtypeStruct((8, B), jnp.int32),
            jax.ShapeDtypeStruct((acts.shape[0], acts.shape[1] + grads_out.shape[1]), BF),
        ),
        in_specs=[HBM, SMEM, HBM, HBM],
        out_specs=(VMEM, SMEM, VMEM, VMEM, VMEM),
        scratch_shapes=[
            pltpu.SMEM(table.shape, jnp.int32),
            pltpu.VMEM((B, B), jnp.int32),
            pltpu.SemaphoreType.DMA((PARTS + 2,)),
        ],
        compiler_params=PARAMS,
        cost_estimate=pl.CostEstimate(flops=0, bytes_accessed=36 * 2**20, transcendentals=0),
        name="grams_away",
    )(
        pltpu.with_memory_space_constraint(table, pltpu.HBM),
        live,
        pltpu.with_memory_space_constraint(acts, pltpu.HBM),
        pltpu.with_memory_space_constraint(grads_out, pltpu.HBM),
    )


def own_grams(table, live, held):
    return pl.pallas_call(
        own_kernel,
        out_shape=GRAMS,
        in_specs=[SMEM, SMEM, VMEM],
        out_specs=VMEM,
        compiler_params=PARAMS,
        cost_estimate=pl.CostEstimate(flops=0, bytes_accessed=18 * 2**20, transcendentals=0),
        name="grams_own",
    )(table, live, held)


def section_kernel(parts_ref, out_ref):
    for row in range(8):
        total = parts_ref[0, row * H : (row + 1) * H, :].astype(F32)
        for g in range(1, 16):
            total += parts_ref[g, row * H : (row + 1) * H, :].astype(F32)
        out_ref[row, :H, :] = total.astype(BF)
    extra = parts_ref[0, 8 * H :, :].astype(F32)
    for g in range(1, 16):
        extra += parts_ref[g, 8 * H :, :].astype(F32)
    count = extra[8:, :]
    high = jnp.floor(count * (1.0 / 256.0))
    low = count - 256.0 * high
    sub = iota((8, B), 0)
    for row in range(8):
        first = jnp.where(sub == 0, jnp.broadcast_to(extra[row : row + 1, :], (8, B)), jnp.where(sub == 1, high, low))
        out_ref[row, H:, :] = jnp.concatenate((first, jnp.zeros_like(first)), axis=0).astype(BF)


def section_sum(parts):
    return pl.pallas_call(
        section_kernel,
        out_shape=jax.ShapeDtypeStruct((8, H + EXTRA, B), BF),
        compiler_params=pltpu.CompilerParams(vmem_limit_bytes=VMEM_LIMIT),
        name="section_sum",
    )(parts)


def take_row(rows, at):
    return jnp.sum(jnp.where(iota((EXTRA, B), 0) == at, rows, 0.0), axis=0, keepdims=True)


def inverse_kernel(parts_ref, old_ref, cov_ref, out_ref):
    half = parts_ref[0, :H, :].astype(F32)
    extra = parts_ref[0, H:, :].astype(F32)
    for s in range(1, 8):
        half += parts_ref[s, :H, :].astype(F32)
        extra += parts_ref[s, H:, :].astype(F32)
    total = extra[1:2, :] * 256.0 + extra[2:3, :]
    gram = unpack(half, extra[:1, :])
    cov = 0.8 * old_ref[0, 0] + 0.2 * gram / total
    cov_ref[0, 0] = cov
    eye = jnp.where(iota((B, B), 0) == iota((B, B), 1), 0.1, 0.0)
    inv_half, inv_diag = pack(invert(cov + eye))
    packed = jnp.concatenate((inv_half, jnp.broadcast_to(inv_diag, (EXTRA, B))), axis=0).astype(BF)
    for section in range(8):
        out_ref[section] = packed


def inverse(parts, old_cov):
    return pl.pallas_call(
        inverse_kernel,
        out_shape=(
            jax.ShapeDtypeStruct(old_cov.shape, F32),
            jax.ShapeDtypeStruct((8, H + EXTRA, B), BF),
        ),
        in_specs=[VMEM, VMEM],
        out_specs=(VMEM, VMEM),
        compiler_params=PARAMS,
        name="inverse",
    )(parts, old_cov)


def route_kernel(room, send_ref, mine_ref, other_ref, out_ref):
    core = lax.axis_index("c")
    for chip in range(16):
        diags = jnp.zeros((EXTRA, B), F32)
        for at in range(room):
            if room in ROOMS:
                index = send_ref[chip, at]
                block = jnp.where(index // 8 == core, mine_ref[index % 8], other_ref[index % 8])
            else:
                block = mine_ref[at]
            out_ref[chip, at * H : (at + 1) * H, :] = block[:H, :]
            diags = jnp.where(iota((EXTRA, B), 0) == at, block[H:, :].astype(F32), diags)
        out_ref[chip, room * H :, :] = diags.astype(BF)


def route(room, sends, mine, other):
    return pl.pallas_call(
        functools.partial(route_kernel, room),
        out_shape=jax.ShapeDtypeStruct((16, room * H + EXTRA, B), BF),
        in_specs=[SMEM, VMEM, VMEM],
        out_specs=VMEM,
        compiler_params=PARAMS,
        name="route",
    )(sends, mine, other)


def pick_kernel(room, col_blocks, find_ref, got_ref, keep_ref, give_ref):
    core = lax.axis_index("c")
    for ref, column in ((keep_ref, core), (give_ref, 1 - core)):
        for want in range(ref.shape[0]):
            index = column * col_blocks + want if want < col_blocks else col_blocks + want
            found = find_ref[0, (8 if room in ROOMS else 32) + index]
            chip, at = found // 16, found % 8
            rows = pl.ds(pl.multiple_of(at * H, H), H)
            ref[want, :H, :] = got_ref[chip, rows, :]
            diag = take_row(got_ref[chip, room * H :, :].astype(F32), at)
            ref[want, H:, :] = jnp.broadcast_to(diag, (EXTRA, B)).astype(BF)


def pick(room, finds, got, row_blocks, col_blocks):
    out = jax.ShapeDtypeStruct((col_blocks + row_blocks, H + EXTRA, B), BF)
    return pl.pallas_call(
        functools.partial(pick_kernel, room, col_blocks),
        out_shape=(out, out),
        in_specs=[SMEM, VMEM],
        out_specs=(VMEM, VMEM),
        compiler_params=PARAMS,
        name="pick",
    )(finds, got)


def final_kernel(find_ref, mine_ref, other_ref, weight_ref, out_ref, left_ref, right_ref, sems):
    core = lax.axis_index("c")
    row_blocks = weight_ref.shape[0] // B
    col_blocks = weight_ref.shape[1] // B

    def block(want, index):
        same = find_ref[0, 56 + index] == core
        packed = jnp.where(same, mine_ref[want], other_ref[want]).astype(F32)
        return unpack(packed[:H, :], packed[H : H + 1, :]).astype(BF)

    col_invs = [block(j, core * col_blocks + j) for j in range(col_blocks)]
    copies = []
    span = row_blocks // STRIPS
    for strip in range(STRIPS):
        for i in range(strip * span, (strip + 1) * span):
            rows = slice(i * B, (i + 1) * B)
            inv = block(col_blocks + i, 2 * col_blocks + i)
            left = jnp.dot(inv, weight_ref[rows, :], preferred_element_type=F32)
            left_ref[rows, :] = left.astype(BF)
        rows = slice(strip * span * B, (strip + 1) * span * B)
        for j in range(col_blocks):
            cols = slice(j * B, (j + 1) * B)
            right = jnp.dot(left_ref[rows, cols], col_invs[j], preferred_element_type=F32)
            right_ref[rows, cols] = right.astype(BF)
        copies.append(pltpu.make_async_copy(right_ref.at[rows, :], out_ref.at[rows, :], sems.at[strip]))
        copies[-1].start()
    for copy in copies:
        copy.wait()


def final(finds, mine, other, weight_grad):
    return pl.pallas_call(
        final_kernel,
        out_shape=jax.ShapeDtypeStruct(weight_grad.shape, BF),
        in_specs=[SMEM, VMEM, VMEM, VMEM],
        out_specs=HBM,
        scratch_shapes=[
            pltpu.VMEM(weight_grad.shape, BF),
            pltpu.VMEM(weight_grad.shape, BF),
            pltpu.SemaphoreType.DMA((STRIPS,)),
        ],
        compiler_params=PARAMS,
        name="final",
    )(finds, mine, other, weight_grad)


def on_device(acts, grads_out, weight_grad, slot_table, row_counts, old_cov):
    row_blocks = weight_grad.shape[0] // B
    col_blocks = weight_grad.shape[1] // B
    plane = ("y", "x")
    exchange = functools.partial(lax.all_to_all, split_axis=0, concat_axis=0, tiled=True)
    swap = functools.partial(lax.ppermute, axis_name="c", perm=[(0, 1), (1, 0)])

    away, branch, sends, finds, held = away_grams(
        slot_table, row_counts, acts, grads_out, row_blocks, col_blocks
    )
    got = swap(away)
    own = own_grams(slot_table, row_counts, held)
    sums = (own.astype(F32) + got.astype(F32)).astype(BF)
    parts = exchange(sums.reshape(16, -1, B), plane)
    parts = exchange(section_sum(parts), "z")
    new_cov, inv = inverse(parts, old_cov)
    mine = exchange(inv, "z")

    def compact(room, sends, finds, mine):
        got = exchange(route(room, sends, mine, swap(mine)), plane)
        return pick(room, finds, got, row_blocks, col_blocks)

    def full(sends, finds, mine):
        got = exchange(route(8, sends, mine, mine), plane)
        return pick(8, finds, got, row_blocks, col_blocks)

    branches = [functools.partial(compact, room) for room in ROOMS] + [full]
    keep, give = lax.switch(branch[0], branches, sends, finds, mine)
    return final(finds, keep, swap(give), weight_grad), new_cov


def solution(mesh):
    wide = Mesh(mesh.devices.reshape(8, 4, 4, 2), ("z", "y", "x", "c"))
    dp = ("y", "x", "c")
    in_specs = (
        P(("z",) + dp, None),
        P(("z",) + dp, None),
        P("z", dp),
        P(),
        P(("z",) + dp),
        P(dp, "z", None, None),
    )
    out_specs = (P("z", dp), P(dp, "z", None, None))
    return jax.shard_map(
        on_device, mesh=wide, in_specs=in_specs, out_specs=out_specs, check_vma=False
    )
```

```python
import functools

import jax
import jax.numpy as jnp
import numpy as np
from jax import lax
from jax.experimental import pallas as pl
from jax.experimental.pallas import tpu as pltpu
from jax.sharding import Mesh, PartitionSpec as P

B = 128
H = B // 2
BF = jnp.bfloat16
F32 = jnp.float32
EXTRA = 16
ROOMS = (5, 6, 8)
Q = H // 2
PARTS = 6
STRIPS = 2
VMEM_LIMIT = 24 * 1024 * 1024


SMEM = pl.BlockSpec(memory_space=pltpu.SMEM)
VMEM = pl.BlockSpec(memory_space=pltpu.VMEM)
HBM = pl.BlockSpec(memory_space=pltpu.HBM)
PARAMS = pltpu.CompilerParams(vmem_limit_bytes=VMEM_LIMIT)


def iota(shape, dim):
    return lax.broadcasted_iota(jnp.int32, shape, dim)


def pack(sym):
    top = sym[:H, :]
    low = pltpu.roll(sym[H:, :], H, 1)
    row, lane = iota((H, B), 0), iota((H, B), 1)
    half = jnp.where(lane < row, low, top)
    diag = jnp.sum(jnp.where(lane == row, low, 0.0), axis=0, keepdims=True)
    return half, diag


def unpack(half, diag):
    row, lane = iota((H, B), 0), iota((H, B), 1)
    upper = jnp.where(lane >= row, half, 0.0)
    lower = jnp.where(lane < row, half, 0.0)
    lower = jnp.where(lane == row, diag, lower)
    lower = pltpu.roll(lower, H, 1)
    part = jnp.concatenate((upper, lower), axis=0)
    brow, blane = iota((B, B), 0), iota((B, B), 1)
    return part + jnp.where(brow == blane, 0.0, part.T)


def eliminate(strips, first, k, m, solve):
    rows = 8
    lane, sub = iota((rows, B), 1), iota((rows, B), 0)
    at, inside = (k - first) // rows, k % rows
    spread = lambda v: jnp.broadcast_to(v, (rows, B))
    cols = [[spread(s[:, k + i : k + i + 1]) for s in strips] for i in range(m)]
    pivot = [[spread(cols[j][at][inside + i : inside + i + 1, :]) for j in range(m)] for i in range(m)]
    inv = solve(pivot)
    lines = [spread(strips[at][inside + i : inside + i + 1, :]) for i in range(m)]
    fresh = []
    for i in range(m):
        line = inv[i][0] * lines[0]
        for j in range(1, m):
            line = line + inv[i][j] * lines[j]
        for j in range(m):
            line = jnp.where(lane == k + j, inv[i][j], line)
        fresh.append(line)
    out = []
    pivots = (lane >= k) & (lane < k + m)
    for g, strip in enumerate(strips):
        new = jnp.where(pivots, 0.0, strip)
        for i in range(m):
            new = new - cols[i][g] * fresh[i]
        if g == at:
            for i in range(m):
                new = jnp.where(sub == inside + i, fresh[i], new)
        out.append(new)
    return out


def solve2(p):
    a, b, c = p[0][0], p[0][1], p[1][1]
    scale = 1.0 / (a * c - b * b)
    off = -b * scale
    return [[c * scale, off], [off, a * scale]]


def solve4(p):
    e = solve2([p[0][:2], p[1][:2]])
    f = [row[2:] for row in p[:2]]
    m = [[e[i][0] * f[0][j] + e[i][1] * f[1][j] for j in range(2)] for i in range(2)]
    s = [[p[2 + i][2 + j] - (f[0][i] * m[0][j] + f[1][i] * m[1][j]) for j in range(2)] for i in range(2)]
    si = solve2(s)
    x = [[m[i][0] * si[0][j] + m[i][1] * si[1][j] for j in range(2)] for i in range(2)]
    top = [[e[i][j] + x[i][0] * m[j][0] + x[i][1] * m[j][1] for j in range(2)] + [-x[i][0], -x[i][1]] for i in range(2)]
    low = [[-x[0][i], -x[1][i]] + si[i] for i in range(2)]
    return top + low


def product(a, b):
    return [[sum(a[i][t] * b[t][j] for t in range(1, len(b))) + a[i][0] * b[0][j] for j in range(len(b[0]))] for i in range(len(a))]


def turned(a):
    return [list(row) for row in zip(*a)]


def solve8(p):
    e = solve4([row[:4] for row in p[:4]])
    f = [row[4:] for row in p[:4]]
    m = product(e, f)
    fm = product(turned(f), m)
    si = solve4([[p[4 + i][4 + j] - fm[i][j] for j in range(4)] for i in range(4)])
    x = product(m, si)
    xm = product(x, turned(m))
    top = [[e[i][j] + xm[i][j] for j in range(4)] + [-x[i][j] for j in range(4)] for i in range(4)]
    low = [[-x[j][i] for j in range(4)] + si[i] for i in range(4)]
    return top + low


def invert(mat):
    size = 32
    dot = functools.partial(jnp.dot, precision=lax.Precision.HIGHEST, preferred_element_type=F32)
    row, lane = iota((B, B), 0), iota((B, B), 1)
    for first in range(0, B, size):
        across = (lane >= first) & (lane < first + size)
        down = (row >= first) & (row < first + size)
        own = jnp.where(across, mat, 0.0)
        strips = [own[first + g : first + g + 8, :] for g in range(0, size, 8)]
        for k in range(first, first + size, 8):
            strips = eliminate(strips, first, k, 8, solve8)
        block = jnp.concatenate(strips, axis=0)
        lines = jnp.where(across[:size], block, dot(block, mat))
        edges = [jnp.zeros((rows, B), F32) for rows in (first, B - first - size)]
        lines = jnp.concatenate([part for part in (edges[0], lines, edges[1]) if part.shape[0]], axis=0)
        mat = jnp.where(down, lines, jnp.where(across, 0.0, mat) - dot(own, lines))
    return mat


def slot_grams(live, want, table_ref, x_ref, out_ref):
    blocks = x_ref.shape[1] // B
    group_rows = 8 * H + EXTRA
    unroll = 8

    @pl.loop(0, 16 // unroll)
    def _(trip):
        for inner in range(unroll):
            group = trip * unroll + inner
            base = pl.multiple_of(group * group_rows, 16)
            diags = jnp.zeros((8, B), F32)
            for row in range(8):
                which = table_ref[(group * 2 + want) * 8 + row]
                filled = jnp.where(which >= 0, live, 0)
                first = pl.multiple_of(jnp.clip(which, 0, blocks - 1) * B, B)
                x = x_ref[:, pl.ds(first, B)]
                x = jnp.where(iota(x.shape, 0) < filled, x, jnp.zeros_like(x))
                gram = lax.dot_general(x, x, (((0,), (0,)), ((), ())), preferred_element_type=F32)
                half, diag = pack(gram)
                out_ref[pl.ds(base + row * H, H), :] = half.astype(BF)
                diags = jnp.where(iota((8, B), 0) == row, diag, diags)
            count = jnp.full((8, B), live, jnp.int32).astype(F32)
            out_ref[pl.ds(base + 8 * H, EXTRA), :] = jnp.concatenate((diags, count), axis=0).astype(BF)


def make_plan(in_blocks, row_blocks, col_blocks, table_ref, branch_ref, send_ref, find_ref, turned_ref):
    chip = lax.axis_index("y") * 4 + lax.axis_index("x")
    wide = 2 * col_blocks
    count = wide + row_blocks
    which, lane = iota((24, B), 0), iota((24, B), 1)
    wanted = jnp.where(
        which < wide,
        in_blocks + (lane % 16) * wide + which,
        jnp.where(which < count, (lane // 16) * row_blocks + which - wide, -2),
    )
    slots = jnp.zeros_like(wanted)
    for slot in range(table_ref.shape[0]):
        slots = jnp.where(wanted == table_ref[slot], slot, slots)
    holder = slots // 16
    ranks = jnp.zeros_like(wanted)
    for at in range(count - 1):
        same = holder == jnp.broadcast_to(holder[at : at + 1, :], holder.shape)
        ranks += jnp.where(same & (which > at), 1, 0)
    most = jnp.max(jnp.where(which < count, ranks, 0))
    sends = jnp.zeros((8, B), jnp.int32)
    for at in range(max(ROOMS)):
        chosen = (holder == chip) & (ranks == at) & (which < count)
        row = jnp.sum(jnp.where(chosen, slots % 16, 0), axis=0, keepdims=True)
        sends = jnp.where(iota((8, B), 0) == at, jnp.broadcast_to(row, (8, B)), sends)
    finds = holder * 8 + ranks
    branch = sum((most >= room).astype(jnp.int32) for room in ROOMS)
    branch_ref[0] = branch
    rest = jnp.zeros((B - 56, B), jnp.int32)
    turned_ref[...] = jnp.concatenate((sends, finds, slots, rest), axis=0).T
    section = lax.axis_index("z") * 16
    send_ref[...] = turned_ref[pl.ds(pl.multiple_of(section, 16), 16), :]
    find_ref[...] = jnp.broadcast_to(turned_ref[pl.ds(section + chip, 1), :], find_ref.shape)


def away_kernel(
    row_blocks, col_blocks, table_ref, live_ref, acts_ref, grads_ref,
    out_ref, branch_ref, send_ref, find_ref, x_ref,
    held_ref, turned_ref, sems,
):
    lookup = pltpu.make_async_copy(table_ref, held_ref, sems.at[PARTS + 1])
    lookup.start()
    inner = acts_ref.shape[1]
    copies = [pltpu.make_async_copy(acts_ref, x_ref.at[:, :inner], sems.at[0])]
    width = grads_ref.shape[1] // PARTS
    for part in range(PARTS):
        source = grads_ref.at[:, part * width : (part + 1) * width]
        target = x_ref.at[:, inner + part * width : inner + (part + 1) * width]
        copies.append(pltpu.make_async_copy(source, target, sems.at[part + 1]))
    for copy in copies:
        copy.start()
    lookup.wait()
    make_plan(acts_ref.shape[1] // B, row_blocks, col_blocks, held_ref, branch_ref, send_ref, find_ref, turned_ref)
    for copy in copies:
        copy.wait()
    slot_grams(live_ref[0], 1 - lax.axis_index("c"), held_ref, x_ref, out_ref)


def own_kernel(table_ref, live_ref, x_ref, out_ref):
    slot_grams(live_ref[0], lax.axis_index("c"), table_ref, x_ref, out_ref)


GRAMS = jax.ShapeDtypeStruct((16 * (8 * H + EXTRA), B), BF)


def away_grams(table, live, acts, grads_out, row_blocks, col_blocks):
    return pl.pallas_call(
        functools.partial(away_kernel, row_blocks, col_blocks),
        out_shape=(
            GRAMS,
            jax.ShapeDtypeStruct((1,), jnp.int32),
            jax.ShapeDtypeStruct((16, B), jnp.int32),
            jax.ShapeDtypeStruct((8, B), jnp.int32),
            jax.ShapeDtypeStruct((acts.shape[0], acts.shape[1] + grads_out.shape[1]), BF),
        ),
        in_specs=[HBM, SMEM, HBM, HBM],
        out_specs=(VMEM, SMEM, VMEM, VMEM, VMEM),
        scratch_shapes=[
            pltpu.SMEM(table.shape, jnp.int32),
            pltpu.VMEM((B, B), jnp.int32),
            pltpu.SemaphoreType.DMA((PARTS + 2,)),
        ],
        compiler_params=PARAMS,
        cost_estimate=pl.CostEstimate(flops=0, bytes_accessed=36 * 2**20, transcendentals=0),
        name="grams_away",
    )(
        pltpu.with_memory_space_constraint(table, pltpu.HBM),
        live,
        pltpu.with_memory_space_constraint(acts, pltpu.HBM),
        pltpu.with_memory_space_constraint(grads_out, pltpu.HBM),
    )


def own_grams(table, live, held):
    return pl.pallas_call(
        own_kernel,
        out_shape=GRAMS,
        in_specs=[SMEM, SMEM, VMEM],
        out_specs=VMEM,
        compiler_params=PARAMS,
        cost_estimate=pl.CostEstimate(flops=0, bytes_accessed=18 * 2**20, transcendentals=0),
        name="grams_own",
    )(table, live, held)


def section_kernel(parts_ref, out_ref):
    for row in range(8):
        total = parts_ref[0, row * H : (row + 1) * H, :].astype(F32)
        for g in range(1, 16):
            total += parts_ref[g, row * H : (row + 1) * H, :].astype(F32)
        out_ref[row, :H, :] = total.astype(BF)
    extra = parts_ref[0, 8 * H :, :].astype(F32)
    for g in range(1, 16):
        extra += parts_ref[g, 8 * H :, :].astype(F32)
    count = extra[8:, :]
    high = jnp.floor(count * (1.0 / 256.0))
    low = count - 256.0 * high
    sub = iota((8, B), 0)
    for row in range(8):
        first = jnp.where(sub == 0, jnp.broadcast_to(extra[row : row + 1, :], (8, B)), jnp.where(sub == 1, high, low))
        out_ref[row, H:, :] = jnp.concatenate((first, jnp.zeros_like(first)), axis=0).astype(BF)


def section_sum(parts):
    return pl.pallas_call(
        section_kernel,
        out_shape=jax.ShapeDtypeStruct((8, H + EXTRA, B), BF),
        compiler_params=pltpu.CompilerParams(vmem_limit_bytes=VMEM_LIMIT),
        name="section_sum",
    )(parts)


def take_row(rows, at):
    return jnp.sum(jnp.where(iota((EXTRA, B), 0) == at, rows, 0.0), axis=0, keepdims=True)


def inverse_kernel(parts_ref, old_ref, cov_ref, out_ref):
    half = parts_ref[0, :H, :].astype(F32)
    extra = parts_ref[0, H:, :].astype(F32)
    for s in range(1, 8):
        half += parts_ref[s, :H, :].astype(F32)
        extra += parts_ref[s, H:, :].astype(F32)
    total = extra[1:2, :] * 256.0 + extra[2:3, :]
    gram = unpack(half, extra[:1, :])
    cov = 0.8 * old_ref[0, 0] + 0.2 * gram / total
    cov_ref[0, 0] = cov
    eye = jnp.where(iota((B, B), 0) == iota((B, B), 1), 0.1, 0.0)
    inv_half, inv_diag = pack(invert(cov + eye))
    packed = jnp.concatenate((inv_half, jnp.broadcast_to(inv_diag, (EXTRA, B))), axis=0).astype(BF)
    for section in range(8):
        out_ref[section] = packed


def inverse(parts, old_cov):
    return pl.pallas_call(
        inverse_kernel,
        out_shape=(
            jax.ShapeDtypeStruct(old_cov.shape, F32),
            jax.ShapeDtypeStruct((8, H + EXTRA, B), BF),
        ),
        in_specs=[VMEM, VMEM],
        out_specs=(VMEM, VMEM),
        compiler_params=PARAMS,
        name="inverse",
    )(parts, old_cov)


def route_kernel(room, send_ref, mine_ref, other_ref, out_ref):
    core = lax.axis_index("c")
    rows = pl.ds(pl.multiple_of(core * Q, Q), Q)
    for chip in range(16):
        diags = jnp.zeros((EXTRA, B), F32)
        for at in range(room):
            index = send_ref[chip, at]
            same = index // 8 == core
            half = jnp.where(same, mine_ref[index % 8, rows, :], other_ref[index % 8, rows, :])
            diag = jnp.where(same, mine_ref[index % 8, H:, :], other_ref[index % 8, H:, :])
            out_ref[chip, at * Q : (at + 1) * Q, :] = half
            diags = jnp.where(iota((EXTRA, B), 0) == at, diag.astype(F32), diags)
        out_ref[chip, room * Q :, :] = diags.astype(BF)


def route(room, sends, mine, other):
    return pl.pallas_call(
        functools.partial(route_kernel, room),
        out_shape=jax.ShapeDtypeStruct((16, room * Q + EXTRA, B), BF),
        in_specs=[SMEM, VMEM, VMEM],
        out_specs=VMEM,
        compiler_params=PARAMS,
        name="route",
    )(sends, mine, other)


def pick_kernel(room, col_blocks, find_ref, got_ref, keep_ref, give_ref):
    core = lax.axis_index("c")
    for ref, column in ((keep_ref, core), (give_ref, 1 - core)):
        for want in range(ref.shape[0]):
            index = column * col_blocks + want if want < col_blocks else col_blocks + want
            found = find_ref[0, 8 + index]
            chip, at = found // 8, found % 8
            ref[want, :Q, :] = got_ref[chip, pl.ds(pl.multiple_of(at * Q, Q), Q), :]
            diag = take_row(got_ref[chip, room * Q :, :].astype(F32), at)
            ref[want, Q:, :] = jnp.broadcast_to(diag, (EXTRA, B)).astype(BF)


def pick_any_kernel(col_blocks, find_ref, mine_ref, other_ref, keep_ref, give_ref):
    core = lax.axis_index("c")
    rows = pl.ds(pl.multiple_of(core * Q, Q), Q)
    for ref, column in ((keep_ref, core), (give_ref, 1 - core)):
        for want in range(ref.shape[0]):
            index = column * col_blocks + want if want < col_blocks else col_blocks + want
            slot = find_ref[0, 32 + index]
            chip, same, at = slot // 16, (slot // 8) % 2 == core, slot % 8
            ref[want, :Q, :] = jnp.where(same, mine_ref[chip, at, rows, :], other_ref[chip, at, rows, :])
            ref[want, Q:, :] = jnp.where(same, mine_ref[chip, at, H:, :], other_ref[chip, at, H:, :])


def pick(kernel, finds, got, row_blocks, col_blocks):
    out = jax.ShapeDtypeStruct((col_blocks + row_blocks, Q + EXTRA, B), BF)
    return pl.pallas_call(
        kernel,
        out_shape=(out, out),
        in_specs=[SMEM] + [VMEM] * len(got),
        out_specs=(VMEM, VMEM),
        compiler_params=PARAMS,
        name="pick",
    )(finds, *got)


def final_kernel(mine_ref, other_ref, weight_ref, out_ref, left_ref, right_ref, sems):
    core = lax.axis_index("c")
    row_blocks = weight_ref.shape[0] // B
    col_blocks = weight_ref.shape[1] // B

    def block(want):
        mine, other = mine_ref[want].astype(F32), other_ref[want].astype(F32)
        first = jnp.where(core == 0, mine[:Q, :], other[:Q, :])
        second = jnp.where(core == 0, other[:Q, :], mine[:Q, :])
        return unpack(jnp.concatenate((first, second), axis=0), mine[Q : Q + 1, :]).astype(BF)

    col_invs = [block(j) for j in range(col_blocks)]
    copies = []
    span = row_blocks // STRIPS
    for strip in range(STRIPS):
        for i in range(strip * span, (strip + 1) * span):
            rows = slice(i * B, (i + 1) * B)
            inv = block(col_blocks + i)
            left = jnp.dot(inv, weight_ref[rows, :], preferred_element_type=F32)
            left_ref[rows, :] = left.astype(BF)
        rows = slice(strip * span * B, (strip + 1) * span * B)
        for j in range(col_blocks):
            cols = slice(j * B, (j + 1) * B)
            right = jnp.dot(left_ref[rows, cols], col_invs[j], preferred_element_type=F32)
            right_ref[rows, cols] = right.astype(BF)
        copies.append(pltpu.make_async_copy(right_ref.at[rows, :], out_ref.at[rows, :], sems.at[strip]))
        copies[-1].start()
    for copy in copies:
        copy.wait()


def final(mine, other, weight_grad):
    return pl.pallas_call(
        final_kernel,
        out_shape=jax.ShapeDtypeStruct(weight_grad.shape, BF),
        in_specs=[VMEM, VMEM, VMEM],
        out_specs=HBM,
        scratch_shapes=[
            pltpu.VMEM(weight_grad.shape, BF),
            pltpu.VMEM(weight_grad.shape, BF),
            pltpu.SemaphoreType.DMA((STRIPS,)),
        ],
        compiler_params=PARAMS,
        name="final",
    )(mine, other, weight_grad)


def on_device(acts, grads_out, weight_grad, slot_table, row_counts, old_cov):
    row_blocks = weight_grad.shape[0] // B
    col_blocks = weight_grad.shape[1] // B
    plane = ("y", "x")
    exchange = functools.partial(lax.all_to_all, split_axis=0, concat_axis=0, tiled=True)
    swap = functools.partial(lax.ppermute, axis_name="c", perm=[(0, 1), (1, 0)])

    away, branch, sends, finds, held = away_grams(
        slot_table, row_counts, acts, grads_out, row_blocks, col_blocks
    )
    got = swap(away)
    own = own_grams(slot_table, row_counts, held)
    sums = (own.astype(F32) + got.astype(F32)).astype(BF)
    parts = exchange(sums.reshape(16, -1, B), plane)
    parts = exchange(section_sum(parts), "z")
    new_cov, inv = inverse(parts, old_cov)
    mine = exchange(inv, "z")

    def compact(room, sends, finds, mine):
        got = exchange(route(room, sends, mine, swap(mine)), plane)
        return pick(functools.partial(pick_kernel, room, col_blocks), finds, (got,), row_blocks, col_blocks)

    def full(sends, finds, mine):
        got = exchange(jnp.broadcast_to(mine[None], (16,) + mine.shape), plane)
        return pick(functools.partial(pick_any_kernel, col_blocks), finds, (got, swap(got)), row_blocks, col_blocks)

    branches = [functools.partial(compact, room) for room in ROOMS] + [full]
    keep, give = lax.switch(branch[0], branches, sends, finds, mine)
    return final(keep, swap(give), weight_grad), new_cov


def solution(mesh):
    wide = Mesh(mesh.devices.reshape(8, 4, 4, 2), ("z", "y", "x", "c"))
    dp = ("y", "x", "c")
    in_specs = (
        P(("z",) + dp, None),
        P(("z",) + dp, None),
        P("z", dp),
        P(),
        P(("z",) + dp),
        P(dp, "z", None, None),
    )
    out_specs = (P("z", dp), P(dp, "z", None, None))
    return jax.shard_map(
        on_device, mesh=wide, in_specs=in_specs, out_specs=out_specs, check_vma=False
    )
```

```python
import functools

import jax
import jax.numpy as jnp
import numpy as np
from jax import lax
from jax.experimental import pallas as pl
from jax.experimental.pallas import tpu as pltpu
from jax.sharding import Mesh, PartitionSpec as P

B = 128
H = B // 2
BF = jnp.bfloat16
F32 = jnp.float32
EXTRA = 16
ROOMS = (5, 6, 8)
Q = H // 2
PARTS = 6
STRIPS = 2
VMEM_LIMIT = 24 * 1024 * 1024


SMEM = pl.BlockSpec(memory_space=pltpu.SMEM)
VMEM = pl.BlockSpec(memory_space=pltpu.VMEM)
HBM = pl.BlockSpec(memory_space=pltpu.HBM)
PARAMS = pltpu.CompilerParams(vmem_limit_bytes=VMEM_LIMIT)


def iota(shape, dim):
    return lax.broadcasted_iota(jnp.int32, shape, dim)


def pack(sym):
    top = sym[:H, :]
    low = pltpu.roll(sym[H:, :], H, 1)
    row, lane = iota((H, B), 0), iota((H, B), 1)
    half = jnp.where(lane < row, low, top)
    diag = jnp.sum(jnp.where(lane == row, low, 0.0), axis=0, keepdims=True)
    return half, diag


def unpack(half, diag):
    row, lane = iota((H, B), 0), iota((H, B), 1)
    upper = jnp.where(lane >= row, half, 0.0)
    lower = jnp.where(lane < row, half, 0.0)
    lower = jnp.where(lane == row, diag, lower)
    lower = pltpu.roll(lower, H, 1)
    part = jnp.concatenate((upper, lower), axis=0)
    brow, blane = iota((B, B), 0), iota((B, B), 1)
    return part + jnp.where(brow == blane, 0.0, part.T)


def eliminate(strips, first, k, m, solve):
    rows = 8
    lane, sub = iota((rows, B), 1), iota((rows, B), 0)
    at, inside = (k - first) // rows, k % rows
    spread = lambda v: jnp.broadcast_to(v, (rows, B))
    cols = [[spread(s[:, k + i : k + i + 1]) for s in strips] for i in range(m)]
    pivot = [[spread(cols[j][at][inside + i : inside + i + 1, :]) for j in range(m)] for i in range(m)]
    inv = solve(pivot)
    lines = [spread(strips[at][inside + i : inside + i + 1, :]) for i in range(m)]
    fresh = []
    for i in range(m):
        line = inv[i][0] * lines[0]
        for j in range(1, m):
            line = line + inv[i][j] * lines[j]
        for j in range(m):
            line = jnp.where(lane == k + j, inv[i][j], line)
        fresh.append(line)
    out = []
    pivots = (lane >= k) & (lane < k + m)
    for g, strip in enumerate(strips):
        new = jnp.where(pivots, 0.0, strip)
        for i in range(m):
            new = new - cols[i][g] * fresh[i]
        if g == at:
            for i in range(m):
                new = jnp.where(sub == inside + i, fresh[i], new)
        out.append(new)
    return out


def solve2(p):
    a, b, c = p[0][0], p[0][1], p[1][1]
    scale = 1.0 / (a * c - b * b)
    off = -b * scale
    return [[c * scale, off], [off, a * scale]]


def solve4(p):
    e = solve2([p[0][:2], p[1][:2]])
    f = [row[2:] for row in p[:2]]
    m = [[e[i][0] * f[0][j] + e[i][1] * f[1][j] for j in range(2)] for i in range(2)]
    s = [[p[2 + i][2 + j] - (f[0][i] * m[0][j] + f[1][i] * m[1][j]) for j in range(2)] for i in range(2)]
    si = solve2(s)
    x = [[m[i][0] * si[0][j] + m[i][1] * si[1][j] for j in range(2)] for i in range(2)]
    top = [[e[i][j] + x[i][0] * m[j][0] + x[i][1] * m[j][1] for j in range(2)] + [-x[i][0], -x[i][1]] for i in range(2)]
    low = [[-x[0][i], -x[1][i]] + si[i] for i in range(2)]
    return top + low


def product(a, b):
    return [[sum(a[i][t] * b[t][j] for t in range(1, len(b))) + a[i][0] * b[0][j] for j in range(len(b[0]))] for i in range(len(a))]


def turned(a):
    return [list(row) for row in zip(*a)]


def solve8(p):
    e = solve4([row[:4] for row in p[:4]])
    f = [row[4:] for row in p[:4]]
    m = product(e, f)
    fm = product(turned(f), m)
    si = solve4([[p[4 + i][4 + j] - fm[i][j] for j in range(4)] for i in range(4)])
    x = product(m, si)
    xm = product(x, turned(m))
    top = [[e[i][j] + xm[i][j] for j in range(4)] + [-x[i][j] for j in range(4)] for i in range(4)]
    low = [[-x[j][i] for j in range(4)] + si[i] for i in range(4)]
    return top + low


def invert(mat):
    size = 32
    dot = functools.partial(jnp.dot, precision=lax.Precision.HIGHEST, preferred_element_type=F32)
    row, lane = iota((B, B), 0), iota((B, B), 1)
    for first in range(0, B, size):
        across = (lane >= first) & (lane < first + size)
        down = (row >= first) & (row < first + size)
        own = jnp.where(across, mat, 0.0)
        strips = [own[first + g : first + g + 8, :] for g in range(0, size, 8)]
        for k in range(first, first + size, 8):
            strips = eliminate(strips, first, k, 8, solve8)
        block = jnp.concatenate(strips, axis=0)
        lines = jnp.where(across[:size], block, dot(block, mat))
        edges = [jnp.zeros((rows, B), F32) for rows in (first, B - first - size)]
        lines = jnp.concatenate([part for part in (edges[0], lines, edges[1]) if part.shape[0]], axis=0)
        mat = jnp.where(down, lines, jnp.where(across, 0.0, mat) - dot(own, lines))
    return mat


def slot_grams(live, want, table_ref, x_ref, out_ref):
    blocks = x_ref.shape[1] // B
    group_rows = 8 * H + EXTRA
    unroll = 8

    @pl.loop(0, 16 // unroll)
    def _(trip):
        for inner in range(unroll):
            group = trip * unroll + inner
            base = pl.multiple_of(group * group_rows, 16)
            diags = jnp.zeros((8, B), F32)
            for row in range(8):
                which = table_ref[(group * 2 + want) * 8 + row]
                filled = jnp.where(which >= 0, live, 0)
                first = pl.multiple_of(jnp.clip(which, 0, blocks - 1) * B, B)
                x = x_ref[:, pl.ds(first, B)]
                x = jnp.where(iota(x.shape, 0) < filled, x, jnp.zeros_like(x))
                gram = lax.dot_general(x, x, (((0,), (0,)), ((), ())), preferred_element_type=F32)
                half, diag = pack(gram)
                out_ref[pl.ds(base + row * H, H), :] = half.astype(BF)
                diags = jnp.where(iota((8, B), 0) == row, diag, diags)
            count = jnp.full((8, B), live, jnp.int32).astype(F32)
            out_ref[pl.ds(base + 8 * H, EXTRA), :] = jnp.concatenate((diags, count), axis=0).astype(BF)


def make_plan(in_blocks, row_blocks, col_blocks, table_ref, branch_ref, send_ref, find_ref, turned_ref):
    chip = lax.axis_index("y") * 4 + lax.axis_index("x")
    wide = 2 * col_blocks
    count = wide + row_blocks
    which, lane = iota((24, B), 0), iota((24, B), 1)
    wanted = jnp.where(
        which < wide,
        in_blocks + (lane % 16) * wide + which,
        jnp.where(which < count, (lane // 16) * row_blocks + which - wide, -2),
    )
    slots = jnp.zeros_like(wanted)
    for slot in range(table_ref.shape[0]):
        slots = jnp.where(wanted == table_ref[slot], slot, slots)
    holder = slots // 16
    ranks = jnp.zeros_like(wanted)
    for at in range(count - 1):
        same = holder == jnp.broadcast_to(holder[at : at + 1, :], holder.shape)
        ranks += jnp.where(same & (which > at), 1, 0)
    most = jnp.max(jnp.where(which < count, ranks, 0))
    sends = jnp.zeros((8, B), jnp.int32)
    for at in range(max(ROOMS)):
        chosen = (holder == chip) & (ranks == at) & (which < count)
        row = jnp.sum(jnp.where(chosen, slots % 16, 0), axis=0, keepdims=True)
        sends = jnp.where(iota((8, B), 0) == at, jnp.broadcast_to(row, (8, B)), sends)
    finds = holder * 8 + ranks
    branch = sum((most >= room).astype(jnp.int32) for room in ROOMS)
    branch_ref[0] = branch
    rest = jnp.zeros((B - 56, B), jnp.int32)
    turned_ref[...] = jnp.concatenate((sends, finds, slots, rest), axis=0).T
    section = lax.axis_index("z") * 16
    send_ref[...] = turned_ref[pl.ds(pl.multiple_of(section, 16), 16), :]
    find_ref[...] = jnp.broadcast_to(turned_ref[pl.ds(section + chip, 1), :], find_ref.shape)


def away_kernel(
    row_blocks, col_blocks, table_ref, live_ref, acts_ref, grads_ref,
    out_ref, branch_ref, send_ref, find_ref, x_ref,
    held_ref, turned_ref, sems,
):
    lookup = pltpu.make_async_copy(table_ref, held_ref, sems.at[PARTS + 1])
    lookup.start()
    inner = acts_ref.shape[1]
    copies = [pltpu.make_async_copy(acts_ref, x_ref.at[:, :inner], sems.at[0])]
    width = grads_ref.shape[1] // PARTS
    for part in range(PARTS):
        source = grads_ref.at[:, part * width : (part + 1) * width]
        target = x_ref.at[:, inner + part * width : inner + (part + 1) * width]
        copies.append(pltpu.make_async_copy(source, target, sems.at[part + 1]))
    for copy in copies:
        copy.start()
    lookup.wait()
    make_plan(acts_ref.shape[1] // B, row_blocks, col_blocks, held_ref, branch_ref, send_ref, find_ref, turned_ref)
    for copy in copies:
        copy.wait()
    slot_grams(live_ref[0], 1 - lax.axis_index("c"), held_ref, x_ref, out_ref)


def own_kernel(table_ref, live_ref, x_ref, out_ref):
    slot_grams(live_ref[0], lax.axis_index("c"), table_ref, x_ref, out_ref)


GRAMS = jax.ShapeDtypeStruct((16 * (8 * H + EXTRA), B), BF)


def away_grams(table, live, acts, grads_out, row_blocks, col_blocks):
    return pl.pallas_call(
        functools.partial(away_kernel, row_blocks, col_blocks),
        out_shape=(
            GRAMS,
            jax.ShapeDtypeStruct((1,), jnp.int32),
            jax.ShapeDtypeStruct((16, B), jnp.int32),
            jax.ShapeDtypeStruct((8, B), jnp.int32),
            jax.ShapeDtypeStruct((acts.shape[0], acts.shape[1] + grads_out.shape[1]), BF),
        ),
        in_specs=[HBM, SMEM, HBM, HBM],
        out_specs=(VMEM, SMEM, VMEM, VMEM, VMEM),
        scratch_shapes=[
            pltpu.SMEM(table.shape, jnp.int32),
            pltpu.VMEM((B, B), jnp.int32),
            pltpu.SemaphoreType.DMA((PARTS + 2,)),
        ],
        compiler_params=PARAMS,
        cost_estimate=pl.CostEstimate(flops=0, bytes_accessed=36 * 2**20, transcendentals=0),
        name="grams_away",
    )(
        pltpu.with_memory_space_constraint(table, pltpu.HBM),
        live,
        pltpu.with_memory_space_constraint(acts, pltpu.HBM),
        pltpu.with_memory_space_constraint(grads_out, pltpu.HBM),
    )


def own_grams(table, live, held):
    return pl.pallas_call(
        own_kernel,
        out_shape=GRAMS,
        in_specs=[SMEM, SMEM, VMEM],
        out_specs=VMEM,
        compiler_params=PARAMS,
        cost_estimate=pl.CostEstimate(flops=0, bytes_accessed=18 * 2**20, transcendentals=0),
        name="grams_own",
    )(table, live, held)


def section_kernel(parts_ref, out_ref):
    for row in range(8):
        total = parts_ref[0, row * H : (row + 1) * H, :].astype(F32)
        for g in range(1, 16):
            total += parts_ref[g, row * H : (row + 1) * H, :].astype(F32)
        out_ref[row, :H, :] = total.astype(BF)
    extra = parts_ref[0, 8 * H :, :].astype(F32)
    for g in range(1, 16):
        extra += parts_ref[g, 8 * H :, :].astype(F32)
    count = extra[8:, :]
    high = jnp.floor(count * (1.0 / 256.0))
    low = count - 256.0 * high
    sub = iota((8, B), 0)
    for row in range(8):
        first = jnp.where(sub == 0, jnp.broadcast_to(extra[row : row + 1, :], (8, B)), jnp.where(sub == 1, high, low))
        out_ref[row, H:, :] = jnp.concatenate((first, jnp.zeros_like(first)), axis=0).astype(BF)


def section_sum(parts):
    return pl.pallas_call(
        section_kernel,
        out_shape=jax.ShapeDtypeStruct((8, H + EXTRA, B), BF),
        compiler_params=pltpu.CompilerParams(vmem_limit_bytes=VMEM_LIMIT),
        name="section_sum",
    )(parts)


def take_row(rows, at):
    return jnp.sum(jnp.where(iota((EXTRA, B), 0) == at, rows, 0.0), axis=0, keepdims=True)


def inverse_kernel(parts_ref, old_ref, cov_ref, out_ref):
    half = parts_ref[0, :H, :].astype(F32)
    extra = parts_ref[0, H:, :].astype(F32)
    for s in range(1, 8):
        half += parts_ref[s, :H, :].astype(F32)
        extra += parts_ref[s, H:, :].astype(F32)
    total = extra[1:2, :] * 256.0 + extra[2:3, :]
    gram = unpack(half, extra[:1, :])
    cov = 0.8 * old_ref[0, 0] + 0.2 * gram / total
    cov_ref[0, 0] = cov
    eye = jnp.where(iota((B, B), 0) == iota((B, B), 1), 0.1, 0.0)
    inv_half, inv_diag = pack(invert(cov + eye))
    packed = jnp.concatenate((inv_half, jnp.broadcast_to(inv_diag, (EXTRA, B))), axis=0).astype(BF)
    for section in range(8):
        out_ref[section] = packed


def inverse(parts, old_cov):
    return pl.pallas_call(
        inverse_kernel,
        out_shape=(
            jax.ShapeDtypeStruct(old_cov.shape, F32),
            jax.ShapeDtypeStruct((8, H + EXTRA, B), BF),
        ),
        in_specs=[VMEM, VMEM],
        out_specs=(VMEM, VMEM),
        compiler_params=PARAMS,
        name="inverse",
    )(parts, old_cov)


def route_kernel(room, send_ref, mine_ref, other_ref, out_ref):
    core = lax.axis_index("c")
    rows = pl.ds(pl.multiple_of(core * Q, Q), Q)
    for chip in range(16):
        diags = jnp.zeros((EXTRA, B), F32)
        for at in range(room):
            index = send_ref[chip, at]
            same = index // 8 == core
            half = jnp.where(same, mine_ref[index % 8, rows, :], other_ref[index % 8, rows, :])
            diag = jnp.where(same, mine_ref[index % 8, H:, :], other_ref[index % 8, H:, :])
            out_ref[chip, at * Q : (at + 1) * Q, :] = half
            diags = jnp.where(iota((EXTRA, B), 0) == at, diag.astype(F32), diags)
        out_ref[chip, room * Q :, :] = diags.astype(BF)


def route(room, sends, mine, other):
    return pl.pallas_call(
        functools.partial(route_kernel, room),
        out_shape=jax.ShapeDtypeStruct((16, room * Q + EXTRA, B), BF),
        in_specs=[SMEM, VMEM, VMEM],
        out_specs=VMEM,
        compiler_params=PARAMS,
        name="route",
    )(sends, mine, other)


def pick_kernel(room, col_blocks, find_ref, got_ref, keep_ref, give_ref):
    core = lax.axis_index("c")
    for ref, column in ((keep_ref, core), (give_ref, 1 - core)):
        for want in range(ref.shape[0]):
            index = column * col_blocks + want if want < col_blocks else col_blocks + want
            found = find_ref[0, 8 + index]
            chip, at = found // 8, found % 8
            ref[want, :Q, :] = got_ref[chip, pl.ds(pl.multiple_of(at * Q, Q), Q), :]
            diag = take_row(got_ref[chip, room * Q :, :].astype(F32), at)
            ref[want, Q:, :] = jnp.broadcast_to(diag, (EXTRA, B)).astype(BF)


def pick_any_kernel(col_blocks, find_ref, mine_ref, other_ref, keep_ref, give_ref):
    core = lax.axis_index("c")
    rows = pl.ds(pl.multiple_of(core * Q, Q), Q)
    for ref, column in ((keep_ref, core), (give_ref, 1 - core)):
        for want in range(ref.shape[0]):
            index = column * col_blocks + want if want < col_blocks else col_blocks + want
            slot = find_ref[0, 32 + index]
            chip, same, at = slot // 16, (slot // 8) % 2 == core, slot % 8
            ref[want, :Q, :] = jnp.where(same, mine_ref[chip, at, rows, :], other_ref[chip, at, rows, :])
            ref[want, Q:, :] = jnp.where(same, mine_ref[chip, at, H:, :], other_ref[chip, at, H:, :])


def pick(kernel, finds, got, row_blocks, col_blocks):
    out = jax.ShapeDtypeStruct((col_blocks + row_blocks, Q + EXTRA, B), BF)
    return pl.pallas_call(
        kernel,
        out_shape=(out, out),
        in_specs=[SMEM] + [VMEM] * len(got),
        out_specs=(VMEM, VMEM),
        compiler_params=PARAMS,
        name="pick",
    )(finds, *got)


def final_kernel(mine_ref, other_ref, weight_ref, out_ref, left_ref, right_ref, sems):
    core = lax.axis_index("c")
    row_blocks = weight_ref.shape[0] // B
    col_blocks = weight_ref.shape[1] // B

    def block(want):
        mine, other = mine_ref[want].astype(F32), other_ref[want].astype(F32)
        first = jnp.where(core == 0, mine[:Q, :], other[:Q, :])
        second = jnp.where(core == 0, other[:Q, :], mine[:Q, :])
        return unpack(jnp.concatenate((first, second), axis=0), mine[Q : Q + 1, :]).astype(BF)

    col_invs = [block(j) for j in range(col_blocks)]
    copies = []
    span = row_blocks // STRIPS
    for strip in range(STRIPS):
        for i in range(strip * span, (strip + 1) * span):
            rows = slice(i * B, (i + 1) * B)
            inv = block(col_blocks + i)
            left = jnp.dot(inv, weight_ref[rows, :], preferred_element_type=F32)
            left_ref[rows, :] = left.astype(BF)
        rows = slice(strip * span * B, (strip + 1) * span * B)
        for j in range(col_blocks):
            cols = slice(j * B, (j + 1) * B)
            right = jnp.dot(left_ref[rows, cols], col_invs[j], preferred_element_type=F32)
            right_ref[rows, cols] = right.astype(BF)
        copies.append(pltpu.make_async_copy(right_ref.at[rows, :], out_ref.at[rows, :], sems.at[strip]))
        copies[-1].start()
    for copy in copies:
        copy.wait()


def final(mine, other, weight_grad):
    return pl.pallas_call(
        final_kernel,
        out_shape=jax.ShapeDtypeStruct(weight_grad.shape, BF),
        in_specs=[VMEM, VMEM, VMEM],
        out_specs=HBM,
        scratch_shapes=[
            pltpu.VMEM(weight_grad.shape, BF),
            pltpu.VMEM(weight_grad.shape, BF),
            pltpu.SemaphoreType.DMA((STRIPS,)),
        ],
        compiler_params=PARAMS,
        name="final",
    )(mine, other, weight_grad)


def on_device(acts, grads_out, weight_grad, slot_table, row_counts, old_cov):
    row_blocks = weight_grad.shape[0] // B
    col_blocks = weight_grad.shape[1] // B
    plane = ("y", "x")
    exchange = functools.partial(lax.all_to_all, split_axis=0, concat_axis=0, tiled=True)
    swap = functools.partial(lax.ppermute, axis_name="c", perm=[(0, 1), (1, 0)])

    away, branch, sends, finds, held = away_grams(
        slot_table, row_counts, acts, grads_out, row_blocks, col_blocks
    )
    got = swap(away)
    own = own_grams(slot_table, row_counts, held)
    sums = (own.astype(F32) + got.astype(F32)).astype(BF)
    parts = exchange(sums.reshape(16, -1, B), plane)
    parts = exchange(section_sum(parts), "z")
    new_cov, inv = inverse(parts, old_cov)

    def compact(room, sends, finds, inv):
        mine = exchange(inv, "z")
        got = exchange(route(room, sends, mine, swap(mine)), plane)
        return pick(functools.partial(pick_kernel, room, col_blocks), finds, (got,), row_blocks, col_blocks)

    def full(sends, finds, inv):
        mine = exchange(inv, "z")
        got = exchange(jnp.broadcast_to(mine[None], (16,) + mine.shape), plane)
        return pick(functools.partial(pick_any_kernel, col_blocks), finds, (got, swap(got)), row_blocks, col_blocks)

    branches = [functools.partial(compact, room) for room in ROOMS] + [full]
    keep, give = lax.switch(branch[0], branches, sends, finds, inv)
    return final(keep, swap(give), weight_grad), new_cov


def solution(mesh):
    wide = Mesh(mesh.devices.reshape(8, 4, 4, 2), ("z", "y", "x", "c"))
    dp = ("y", "x", "c")
    in_specs = (
        P(("z",) + dp, None),
        P(("z",) + dp, None),
        P("z", dp),
        P(),
        P(("z",) + dp),
        P(dp, "z", None, None),
    )
    out_specs = (P("z", dp), P(dp, "z", None, None))
    return jax.shard_map(
        on_device, mesh=wide, in_specs=in_specs, out_specs=out_specs, check_vma=False
    )
```
